128 devices in a mesh: seq: 32 (over x, y_lo, z), mp: 4 (over y_hi, core).
Axes of the slice: x: 4, y: 4 (y_hi: 2, y_lo: 2; y = y_hi * 2 + y_lo), z: 4, core: 2. Of those that a mesh axis runs over, the one named last changes fastest.
Arguments:
- tokens: bfloat16 [16384, 5376], P('seq', 'mp'), may hold values from -6 to 6
- gain_pre: float32 [5376], replicated, may hold values from 0.1 to 1.9
- w_query: bfloat16 [5376, 2048], P(None, 'mp'), may hold values from -1 to 1
- w_key: bfloat16 [5376, 1024], P(None, 'mp'), may hold values from -1 to 1
- w_value: bfloat16 [5376, 1024], P(None, 'mp'), may hold values from -0.078125 to 0.078125
- w_out: bfloat16 [2048, 5376], P('mp'), may hold values from -0.1875 to 0.1875
- gain_post: float32 [5376], P('mp'), may hold values from 0.1 to 1.9
- prefix_cache: bfloat16 [8, 4096, 2, 1024], P(None, 'seq', None, 'mp'), may hold values from -6 to 6
- template_ids: int32 [4], replicated, may hold values from 0 to 7
- prefix_lengths: int32 [8], replicated, may hold values from 1 to 4096, as said below
- doc_lengths: int32 [4], replicated, may hold values from 1024 to 4096, as said below
Outputs:
- mixed: bfloat16 [16384, 5376], P('seq', 'mp')
The draws below stay inside these ranges and needn't reach their ends.
Inputs may be any that keep to these rules, and one draw needn't show every extreme that they name: `prefix_lengths`: some template has all 4096 positions. `doc_lengths`: the last document fills all 4096 slots.
All inputs are finite; a program needn't handle non-finite values.
Results may differ from the reference program's by a relative error of at most 0.014.
Values may be sent and summed in bfloat16 or wider, within the bound.
No kernel may reach another device: no remote copies, remote signals or barrier semaphores. Data moves between devices by JAX's collectives and lax.ppermute only.
A program may use at most 128 MiB of HBM per device.

```python
import jax
import jax.numpy as jnp
from jax import lax

D = 5376
HEADS = 16
KV_HEADS = 8
HEAD_DIM = 128
WINDOW = 1024
DOCS = 4
NTPL = 8
TOK_DEV = 512
TOKENS = 16384
DOC_LEN = 4096
PREFIX = 4096
N_MP = 4


def draw_w_query(key, part):
    key = jax.random.fold_in(key, 1)
    fresh_part = jax.random.normal(key, (D, HEADS * HEAD_DIM), jnp.float32) / jnp.sqrt(float(D))
    return jnp.clip(fresh_part, -1.0, 1.0).astype(jnp.bfloat16)


def draw_w_key(key, part):
    key = jax.random.fold_in(key, 2)
    fresh_part = jax.random.normal(key, (D, KV_HEADS * HEAD_DIM), jnp.float32) / jnp.sqrt(float(D))
    return jnp.clip(fresh_part, -1.0, 1.0).astype(jnp.bfloat16)


def draw_prefix_lengths(key, part):
    key = jax.random.fold_in(key, 3)
    first_key, second_key = jax.random.split(key)
    lengths = jax.random.randint(first_key, (NTPL,), 1, PREFIX + 1)
    chosen_slot = jax.random.randint(second_key, (), 0, NTPL)
    return jnp.where(jnp.arange(NTPL) == chosen_slot, PREFIX, lengths).astype(jnp.int32)


def draw_doc_lengths(key, part):
    key = jax.random.fold_in(key, 4)
    lengths = jax.random.randint(key, (DOCS,), DOC_LEN // 4, DOC_LEN + 1)
    return jnp.where(jnp.arange(DOCS) == DOCS - 1, DOC_LEN, lengths).astype(jnp.int32)


def set_ends(array, stream_key, smallest, high):
    index_at = [jax.random.randint(jax.random.fold_in(stream_key, axis), (), 0, length) for axis, length in enumerate(array.shape)]
    main_axis = array.shape.index(max(array.shape))
    beside = index_at[:main_axis] + [(index_at[main_axis] + 1) % array.shape[main_axis]] + index_at[main_axis + 1:]
    return array.at[tuple(index_at)].set(smallest).at[tuple(beside)].set(high)


def strengthened(values, own_key, source, target, shards_of, factor):
    owner, partner = [(jnp.arange(values.shape[axis_at]) // (values.shape[axis_at] // shards_of)).reshape([-1 if axis == axis_at else 1 for axis in range(values.ndim)]) for axis_at in (source, target)]
    chosen = jax.random.permutation(own_key, shards_of)[partner]
    strong = (owner == chosen) | (owner == (partner + shards_of // 2) % shards_of)
    return jnp.where(strong, factor * values, values)


def level_of(own_key, shape, pieces, low, largest):
    gain = 1.0
    for position, parts in pieces:
        draws = jax.random.uniform(jax.random.fold_in(jax.random.fold_in(own_key, 6), position), (parts,), jnp.float32, low / len(pieces), largest / len(pieces))
        gain = gain * jnp.repeat(jnp.exp(draws), shape[position] // parts).reshape((-1,) + (1,) * (len(shape) - 1 - position))
    return gain


def gaussian(rng, shape, deviation, reach, shards=(), held_as=jnp.bfloat16):
    loudness = level_of(rng, shape, shards, -0.22, 0.18) if shards else 1.0
    values = jax.random.normal(rng, shape, jnp.float32) * deviation * loudness
    return jnp.minimum(jnp.maximum(values, -reach), reach).astype(held_as)


def bell_draw_with(stream_key, shape, spread, reach, pieces, heavy, dtype=jnp.bfloat16):
    result = spread * jax.random.normal(stream_key, shape, jnp.float32)
    if pieces:
        result = result * level_of(stream_key, shape, pieces, -0.22, 0.18)
    return jnp.clip(strengthened(result, jax.random.fold_in(stream_key, 3), *heavy), -reach, reach).astype(dtype)


def setup_inputs(seed: int = 0) -> dict:
    streams_of = jax.random.split(jax.random.key(seed), 12)
    tokens = gaussian(streams_of[0], (TOKENS, D), 1.0, 6.0, ((0, 32), (1, 4)))
    gain_pre = jnp.clip(1.0 + 0.18 * jax.random.normal(streams_of[1], (D,), jnp.float32), 0.1, 1.9)
    w_query = draw_w_query(jax.random.fold_in(streams_of[11], 71), 0)
    w_key = draw_w_key(jax.random.fold_in(streams_of[11], 71), 0)
    w_value = gaussian(streams_of[4], (D, KV_HEADS * HEAD_DIM), D ** -0.5, 0.078125, ((1, 4),))
    w_out = bell_draw_with(streams_of[5], (HEADS * HEAD_DIM, D), (HEADS * HEAD_DIM) ** -0.5, 0.1875, ((0, 4),), (0, 1, 4, 2.0))
    gain_post = jnp.clip(1.0 + 0.18 * jax.random.normal(streams_of[6], (D,), jnp.float32), 0.1, 1.9)
    prefix_cache = gaussian(streams_of[7], (NTPL, PREFIX, 2, KV_HEADS * HEAD_DIM), 1.0, 6.0, ((1, 32), (3, 4)))
    template_ids = set_ends(jax.random.randint(streams_of[8], (DOCS,), 0, NTPL), jax.random.fold_in(streams_of[8], 1), 0, NTPL - 1).astype(jnp.int32)
    prefix_lengths = draw_prefix_lengths(jax.random.fold_in(streams_of[11], 71), 0)
    doc_lengths = draw_doc_lengths(jax.random.fold_in(streams_of[11], 71), 0)
    return {"tokens": tokens, "gain_pre": gain_pre, "w_query": w_query, "w_key": w_key, "w_value": w_value, "w_out": w_out, "gain_post": gain_post, "prefix_cache": prefix_cache, "template_ids": template_ids, "prefix_lengths": prefix_lengths, "doc_lengths": doc_lengths}


epsilon = 1e-06
query_scalar = 168.0
rope_base = 10000.0

def rotate(values, places):
    half_dim = values.shape[-1] // 2
    frequency = rope_base ** (-(jnp.arange(half_dim).astype(jnp.float32) * 2.0 / values.shape[-1]))
    angles = places.astype(jnp.float32)[:, None] * frequency[None, :]
    cosine = jnp.cos(angles)[:, None, :]
    sine_part = jnp.sin(angles)[:, None, :]
    first_half = values[..., :half_dim]
    second_half = values[..., half_dim:]
    return jnp.concatenate([first_half * cosine - second_half * sine_part, second_half * cosine + first_half * sine_part], -1)

def window_mask(query_index, query_pos, prefix_len, doc_len, prefix_count, key_index, window_size):
    prefix_pos = jnp.arange(prefix_count).astype(jnp.int32)
    prefix_ok = prefix_pos < prefix_len
    doc_ok = (key_index >= 0) & (key_index < doc_len)
    key_pos = jnp.concatenate([prefix_pos, prefix_len + key_index])
    key_ok = jnp.concatenate([prefix_ok, doc_ok])
    distance = query_pos[:, None] - key_pos[None, :]
    inside = key_ok[None, :] & (distance >= 0) & (distance < window_size)
    own_index = jnp.concatenate([jnp.full((prefix_count,), -1, jnp.int32), key_index])
    self_pair = (own_index[None, :] == query_index[:, None]) & (own_index[None, :] >= 0)
    return inside | self_pair

def attend(queries, keys_all, values_all, allowed):
    scores = jnp.einsum('rkgd,nkd->kgrn', queries.astype(jnp.float32), keys_all.astype(jnp.float32), precision=lax.Precision.HIGHEST)
    scores = jnp.where(allowed[None, None], scores, -1e+30)
    highest = lax.optimization_barrier(jnp.max(scores, -1, keepdims=True))
    weights = jnp.exp(scores - highest)
    totals = lax.optimization_barrier(jnp.sum(weights, -1))
    rounded = weights.astype(jnp.bfloat16).astype(jnp.float32)
    context = jnp.einsum('kgrn,nkd->rkgd', rounded, values_all.astype(jnp.float32), precision=lax.Precision.HIGHEST)
    return context / jnp.transpose(totals, (2, 0, 1))[..., None]

def reference(tokens, gain_pre, w_query, w_key, w_value, w_out, gain_post, prefix_cache, template_ids, prefix_lengths, doc_lengths):
    floated = tokens.astype(jnp.float32)
    normed = (floated * lax.rsqrt(lax.optimization_barrier(jnp.mean(floated * floated, 1, keepdims=True)) + epsilon) * gain_pre).astype(jnp.bfloat16)
    token_rows = jnp.arange(TOKENS).astype(jnp.int32)
    doc_number = token_rows // DOC_LEN
    doc_index = token_rows % DOC_LEN
    positions = prefix_lengths[template_ids[doc_number]] + doc_index
    queries = rotate(jnp.dot(normed, w_query, preferred_element_type=jnp.float32).reshape(TOKENS, HEADS, HEAD_DIM), positions)
    queries = (queries * query_scalar ** (-0.5)).astype(jnp.bfloat16)
    keys = rotate(jnp.dot(normed, w_key, preferred_element_type=jnp.float32).reshape(TOKENS, KV_HEADS, HEAD_DIM), positions)
    keys = keys.astype(jnp.bfloat16).reshape(TOKENS, KV_HEADS * HEAD_DIM)
    values = jnp.dot(normed, w_value, preferred_element_type=jnp.float32).astype(jnp.bfloat16)
    pairs = jnp.stack([keys, values], 1)
    padded = jnp.concatenate([jnp.zeros((WINDOW, 2, KV_HEADS * HEAD_DIM), jnp.bfloat16), pairs], 0)
    group_size = HEADS // KV_HEADS

    def one_block(block_number):
        block_start = (block_number * TOK_DEV).astype(jnp.int32)
        block_queries = lax.dynamic_slice_in_dim(queries, block_start, TOK_DEV, 0).reshape(TOK_DEV, KV_HEADS, group_size, HEAD_DIM)
        block_pairs = lax.dynamic_slice_in_dim(padded, block_start, WINDOW + TOK_DEV, 0)
        document = block_start // DOC_LEN
        template = template_ids[document]
        prefix_len = prefix_lengths[template]
        doc_len = doc_lengths[document]
        query_index = block_start - document * DOC_LEN + jnp.arange(TOK_DEV).astype(jnp.int32)
        query_pos = prefix_len + query_index
        key_index = block_start - WINDOW - document * DOC_LEN + jnp.arange(WINDOW + TOK_DEV).astype(jnp.int32)
        prefix_pair = prefix_cache[template]
        allowed = window_mask(query_index, query_pos, prefix_len, doc_len, PREFIX, key_index, WINDOW)
        keys_all = jnp.concatenate([prefix_pair[:, 0], block_pairs[:, 0]], 0).reshape(-1, KV_HEADS, HEAD_DIM)
        values_all = jnp.concatenate([prefix_pair[:, 1], block_pairs[:, 1]], 0).reshape(-1, KV_HEADS, HEAD_DIM)
        context = attend(block_queries, keys_all, values_all, allowed)
        context = jnp.where((query_index < doc_len)[:, None, None, None], context, 0.0)
        return context.astype(jnp.bfloat16).reshape(TOK_DEV, HEADS * HEAD_DIM)
    context = lax.map(one_block, jnp.arange(TOKENS // TOK_DEV).astype(jnp.int32)).reshape(TOKENS, HEADS * HEAD_DIM)
    group_width = HEADS * HEAD_DIM // N_MP
    attended = jnp.zeros((TOKENS, D), jnp.float32)
    for member in range(N_MP):
        group_term = jnp.dot(context[:, member * group_width:(member + 1) * group_width], w_out[member * group_width:(member + 1) * group_width], preferred_element_type=jnp.float32).astype(jnp.bfloat16)
        attended = attended + lax.optimization_barrier(group_term).astype(jnp.float32)
    squares = lax.optimization_barrier(jnp.mean(attended * attended, 1, keepdims=True))
    return (floated + gain_post * attended * lax.rsqrt(squares + epsilon)).astype(jnp.bfloat16)
```

```python
import functools

import jax
import jax.numpy as jnp
from jax import lax
from jax.experimental import pallas as pl
from jax.experimental.pallas import tpu as pltpu
from jax.sharding import PartitionSpec as P

HEAD_DIM = 128
WINDOW = 1024
DOCS = 4
MP = 4
ROWS = 512
FEATURES = 1344
HEADS_LOCAL = 4
KV_WIDTH = 256
PAIR = 2 * KV_WIDTH
DOC_SHARDS = 8
HELD = 128
VMEM_LIMIT = 56 * 1024 * 1024

epsilon = 1e-06
query_scalar = 168.0
rope_base = 10000.0
F32 = jnp.float32
BF16 = jnp.bfloat16


def cost(flops, moved, exps=0):
    return pl.CostEstimate(flops=flops, bytes_accessed=moved, transcendentals=exps)


def params():
    return pltpu.CompilerParams(vmem_limit_bytes=VMEM_LIMIT)


def across_mp(array, flip):
    return lax.ppermute(array, "mp", [(i, i ^ flip) for i in range(MP)])


def seq_place(x, y_lo, z):
    return x * 8 + y_lo * 4 + z


def along_x(array, by):
    pairs = [
        (seq_place(x, y, z), seq_place((x + by) % 4, y, z))
        for x in range(4)
        for y in range(2)
        for z in range(4)
    ]
    return lax.ppermute(array, "seq", pairs)


def to_lower_twin(array):
    pairs = [(seq_place(x, 1, z), seq_place(x, 0, z)) for x in range(4) for z in range(4)]
    return lax.ppermute(array, "seq", pairs)


def within_doc(array, by):
    pairs = [
        (d * DOC_SHARDS + i, d * DOC_SHARDS + i + by)
        for d in range(DOCS)
        for i in range(DOC_SHARDS - by)
    ]
    return lax.ppermute(array, "seq", pairs)


def project_kernel(first, last, order, *refs):
    step = pl.program_id(0)
    x_refs, refs = refs[:2], refs[2:]
    gain, wq, wk, wv = refs[:4]
    refs = refs[4:]
    if first:
        acc, squares = refs
    else:
        acc_in, squares_in, cosine, sine, q_ref, kv_ref, acc, squares = refs

    @pl.when(step == 0)
    def _():
        if first:
            acc[...] = jnp.zeros_like(acc)
            squares[...] = jnp.zeros_like(squares)
        else:
            acc[...] = acc_in[...]
            squares[...] = squares_in[...]

    for number in range(2):

        @pl.when(step == number)
        def _(x_ref=x_refs[number]):
            x = x_ref[...].astype(F32)
            squares[...] += jnp.broadcast_to(jnp.sum(x * x, 1, keepdims=True), squares.shape)
            scaled = (x * gain[0]).astype(BF16)
            acc[:, :512] += jnp.dot(scaled, wq[...], preferred_element_type=F32)
            acc[:, 512:768] += jnp.dot(scaled, wk[...], preferred_element_type=F32)
            acc[:, 768:] += jnp.dot(scaled, wv[...], preferred_element_type=F32)

    if last:

        @pl.when(step == 1)
        def _():
            scale = lax.rsqrt(squares[...] * (1.0 / (MP * FEATURES)) + epsilon)
            cos_all = cosine[...]
            sin_all = sine[...]
            for head in range(6):
                cols = slice(head * HEAD_DIM, (head + 1) * HEAD_DIM)
                part = acc[:, cols] * scale
                turned = part * cos_all + pltpu.roll(part, 64, 1) * sin_all
                if head < HEADS_LOCAL:
                    q_ref[:, cols] = (turned * query_scalar ** (-0.5)).astype(BF16)
                else:
                    at = (head - HEADS_LOCAL) * HEAD_DIM
                    kv_ref[:, at : at + HEAD_DIM] = turned.astype(BF16)
            kv_ref[:, KV_WIDTH : KV_WIDTH + HEAD_DIM] = (acc[:, 768:896] * scale).astype(BF16)
            kv_ref[:, KV_WIDTH + HEAD_DIM :] = (acc[:, 896:] * scale).astype(BF16)


def project(order, xs, gain, wq, wk, wv, carried=None, tables=None):
    first = carried is None
    full = lambda shape: pl.BlockSpec(shape, lambda i, order: (0,) * len(shape))
    chunk = lambda width: pl.BlockSpec((FEATURES, width), lambda i, order: (order[i], 0))
    in_specs = [full((ROWS, FEATURES))] * 2 + [
        pl.BlockSpec((1, 1, FEATURES), lambda i, order: (order[i], 0, 0)),
        chunk(512),
        chunk(256),
        chunk(256),
    ]
    args = [*xs, gain, wq, wk, wv]
    acc_shape = [(ROWS, 1024), (ROWS, HEAD_DIM)]
    if first:
        out_shape = [jax.ShapeDtypeStruct(s, F32) for s in acc_shape]
        out_specs = [full(s) for s in acc_shape]
        scratch = []
    else:
        in_specs += [full(s) for s in acc_shape] + [full((ROWS, HEAD_DIM))] * 2
        args += [*carried, *tables]
        out_shape = [jax.ShapeDtypeStruct((ROWS, 512), BF16)] * 2
        out_specs = [full((ROWS, 512))] * 2
        scratch = [pltpu.VMEM(s, F32) for s in acc_shape]
    return pl.pallas_call(
        functools.partial(project_kernel, first, not first),
        grid_spec=pltpu.PrefetchScalarGridSpec(
            num_scalar_prefetch=1,
            grid=(2,),
            in_specs=in_specs,
            out_specs=out_specs,
            scratch_shapes=scratch,
        ),
        out_shape=out_shape,
        compiler_params=params(),
        cost_estimate=cost(2 * ROWS * 2 * FEATURES * 1024, 11_000_000),
    )(order, *args)


def attention_kernel(info, q_ref, own, one_back, two_back, prefix, out, held, sems):
    local = info[0]
    length = info[1]
    real = info[2]

    def copies(branch):
        got = []
        if branch == 0:
            got += [(prefix.at[z, 0], held.at[pl.ds(z * HELD, HELD)]) for z in range(4)]
            got += [(prefix.at[z, 1], held.at[pl.ds(ROWS + z * HELD, HELD)]) for z in range(4)]
        elif branch == 1:
            got += [(prefix.at[z, 1], held.at[pl.ds(z * HELD, HELD)]) for z in range(4)]
            got += [(one_back, held.at[pl.ds(ROWS, ROWS)])]
        else:
            got += [(two_back, held.at[pl.ds(0, ROWS)]), (one_back, held.at[pl.ds(ROWS, ROWS)])]
        return [pltpu.make_async_copy(a, b, sems.at[i]) for i, (a, b) in enumerate(got)]

    for branch in range(3):

        @pl.when(local == branch if branch < 2 else local >= 2)
        def _(branch=branch):
            started = copies(branch)
            for one in started:
                one.start()
            for one in started:
                one.wait()

    column = lax.broadcasted_iota(jnp.int32, (1, ROWS), 1)
    shift_two = jnp.where(local < 2, length, 0)
    limit_two = jnp.where(local < 2, WINDOW - ROWS * local - length, 0)
    shift_one = jnp.where(local < 1, length, 0)
    limit_one = jnp.where(local < 1, ROWS - length, 0)
    place_two = (column - shift_two) & (ROWS - 1)
    place_one = (column - shift_one) & (ROWS - 1)
    one_ok = place_one >= limit_one
    dims = (((1,), (1,)), ((), ()))
    block = 128
    for chunk in range(ROWS // block):
        row = chunk * block + lax.broadcasted_iota(jnp.int32, (block, 1), 0)
        two_ok = place_two > jnp.maximum(row, limit_two - 1)
        reach = (chunk + 1) * block
        own_ok = column[:, :reach] <= row
        row_real = row + local * ROWS < real
        for head in range(HEADS_LOCAL):
            k_cols = slice((head // 2) * HEAD_DIM, (head // 2 + 1) * HEAD_DIM)
            v_cols = slice(KV_WIDTH + k_cols.start, KV_WIDTH + k_cols.stop)
            cols = slice(head * HEAD_DIM, (head + 1) * HEAD_DIM)
            q = q_ref[chunk * block : reach, cols]
            s_two = lax.dot_general(q, held[:ROWS, k_cols], dims, preferred_element_type=F32)
            s_one = lax.dot_general(q, held[ROWS:, k_cols], dims, preferred_element_type=F32)
            s_own = lax.dot_general(q, own[:reach, k_cols], dims, preferred_element_type=F32)
            s_two = jnp.where(two_ok, s_two, -1e30)
            s_one = jnp.where(one_ok, s_one, -1e30)
            s_own = jnp.where(own_ok, s_own, -1e30)
            top = jnp.maximum(
                jnp.maximum(
                    jnp.max(s_two, 1, keepdims=True), jnp.max(s_one, 1, keepdims=True)
                ),
                jnp.max(s_own, 1, keepdims=True),
            )
            w_two = jnp.exp(s_two - top)
            w_one = jnp.exp(s_one - top)
            w_own = jnp.exp(s_own - top)
            total = (
                jnp.sum(w_two, 1, keepdims=True)
                + jnp.sum(w_one, 1, keepdims=True)
                + jnp.sum(w_own, 1, keepdims=True)
            )
            got = (
                jnp.dot(w_two.astype(BF16), held[:ROWS, v_cols], preferred_element_type=F32)
                + jnp.dot(w_one.astype(BF16), held[ROWS:, v_cols], preferred_element_type=F32)
                + jnp.dot(w_own.astype(BF16), own[:reach, v_cols], preferred_element_type=F32)
            )
            got = jnp.where(row_real, got / total, 0.0)
            out[chunk * block : reach, cols] = got.astype(BF16)


def attention(info, q, own, one_back, two_back, prefix):
    full = pl.BlockSpec((ROWS, 512), lambda i, info: (0, 0))
    anywhere = pl.BlockSpec(memory_space=pl.ANY)
    return pl.pallas_call(
        attention_kernel,
        grid_spec=pltpu.PrefetchScalarGridSpec(
            num_scalar_prefetch=1,
            grid=(1,),
            in_specs=[full, full, anywhere, anywhere, anywhere],
            out_specs=full,
            scratch_shapes=[
                pltpu.VMEM((2 * ROWS, PAIR), BF16),
                pltpu.SemaphoreType.DMA((8,)),
            ],
        ),
        out_shape=jax.ShapeDtypeStruct((ROWS, 512), BF16),
        compiler_params=params(),
        cost_estimate=cost(4 * HEADS_LOCAL * ROWS * 1536 * 128, 3_000_000, HEADS_LOCAL * ROWS * 1536),
    )(info, q, own, one_back, two_back, prefix)


def output_kernel(c0, c1, c2, c3, w0, w1, w2, w3, attended, squares):
    total = jnp.dot(c0[...], w0[...], preferred_element_type=F32)
    total += jnp.dot(c1[...], w1[...], preferred_element_type=F32)
    total += jnp.dot(c2[...], w2[...], preferred_element_type=F32)
    total += jnp.dot(c3[...], w3[...], preferred_element_type=F32)
    attended[...] = total
    squares[...] = jnp.broadcast_to(jnp.sum(total * total, 1, keepdims=True), squares.shape)


def output(contexts, weights):
    block = 256
    rows = pl.BlockSpec((block, 512), lambda i: (i, 0))
    full = pl.BlockSpec((512, FEATURES), lambda i: (0, 0))
    return pl.pallas_call(
        output_kernel,
        grid=(ROWS // block,),
        in_specs=[rows] * 4 + [full] * 4,
        out_specs=[
            pl.BlockSpec((block, FEATURES), lambda i: (i, 0)),
            pl.BlockSpec((block, HEAD_DIM), lambda i: (i, 0)),
        ],
        out_shape=[
            jax.ShapeDtypeStruct((ROWS, FEATURES), F32),
            jax.ShapeDtypeStruct((ROWS, HEAD_DIM), F32),
        ],
        compiler_params=params(),
        cost_estimate=cost(2 * ROWS * 2048 * FEATURES, 11_000_000),
    )(*contexts, *weights)


def rope_tables(places):
    lane = jnp.arange(HEAD_DIM)
    frequency = rope_base ** (-((lane % 64).astype(F32) * 2.0 / HEAD_DIM))
    angles = places.astype(F32)[:, None] * frequency[None, :]
    return jnp.cos(angles), jnp.where(lane[None, :] < 64, -jnp.sin(angles), jnp.sin(angles))


def shards(
    tokens,
    gain_pre,
    w_query,
    w_key,
    w_value,
    w_out,
    gain_post,
    prefix_cache,
    template_ids,
    prefix_lengths,
    doc_lengths,
):
    member = lax.axis_index("mp")
    place = lax.axis_index("seq")
    doc = place // DOC_SHARDS
    local = place % DOC_SHARDS
    z_place = place % 4
    length = prefix_lengths[template_ids[doc]]

    far = across_mp(tokens, 2)
    near = across_mp(tokens, 1)

    piece = (place // DOC_SHARDS) * 4 + z_place

    def block_for(flip, start, count):
        return lax.dynamic_slice(w_out, (start, (member ^ flip) * FEATURES), (count, FEATURES))

    w_own = block_for(0, 0, 512)
    w_near = across_mp(block_for(1, 0, 512), 1)
    w_pieces = jnp.stack(
        [across_mp(block_for(2, piece * 32, 32), 2), across_mp(block_for(3, piece * 32, 32), 3)]
    )
    groups = [[seq_place(x, y, z) for x in range(4) for z in range(4)] for y in range(2)]
    w_far = lax.all_gather(w_pieces, "seq", axis=1, tiled=True, axis_index_groups=groups)

    held_at = place * HELD + jnp.arange(HELD)

    def masked_rows(document):
        template = template_ids[document]
        reach = prefix_lengths[template]
        rows = lax.dynamic_index_in_dim(prefix_cache, template, 0, False).reshape(HELD, PAIR)
        wanted = (held_at < reach) & (held_at >= reach - WINDOW)
        return jnp.where(wanted[:, None], rows, jnp.zeros((), BF16))

    mine = masked_rows(doc)
    for by in range(1, 4):
        mine = mine + along_x(masked_rows((doc + by) % DOCS), by)
    twin = to_lower_twin(mine)
    mine_late = ((z_place * HELD + jnp.arange(HELD) - length) & (WINDOW - 1)) >= ROWS
    ordered = jnp.stack(
        [
            jnp.where(mine_late[:, None], twin, mine),
            jnp.where(mine_late[:, None], mine, twin),
        ]
    )
    z_groups = [[seq_place(x, y, z) for z in range(4)] for x in range(4) for y in range(2)]
    prefix = lax.all_gather(ordered[None], "seq", axis=0, tiled=True, axis_index_groups=z_groups)

    tables = rope_tables(length + local * ROWS + jnp.arange(ROWS))
    gain = gain_pre.reshape(MP, 1, FEATURES)
    order = jnp.stack([member, member ^ 1, member ^ 2, member ^ 3]).astype(jnp.int32)
    carried = project(order[:2], [tokens, near], gain, w_query, w_key, w_value)
    far_near = across_mp(far, 1)
    queries, own = project(
        order[2:], [far, far_near], gain, w_query, w_key, w_value, carried, tables
    )
    one_back = within_doc(own, 1)
    two_back = within_doc(own, 2)
    info = jnp.stack([local, length, doc_lengths[doc]]).astype(jnp.int32)
    context = attention(info, queries, own, one_back, two_back, prefix)
    c_far = across_mp(context, 2)
    c_near = across_mp(context, 1)
    c_far_near = across_mp(c_far, 1)
    attended, squares = output(
        [context, c_near, c_far, c_far_near], [w_own, w_near, w_far[0], w_far[1]]
    )
    own_squares = squares[:, 0]
    total = own_squares
    for flip in (1, 2, 3):
        total = total + across_mp(own_squares, flip)
    scale = lax.rsqrt(total * (1.0 / (MP * FEATURES)) + epsilon)
    return (tokens.astype(F32) + gain_post * attended * scale[:, None]).astype(BF16)


def solution(mesh):
    placed = (
        P("seq", "mp"),
        P(),
        P(None, "mp"),
        P(None, "mp"),
        P(None, "mp"),
        P("mp", None),
        P("mp"),
        P(None, "seq", None, "mp"),
        P(),
        P(),
        P(),
    )
    return jax.shard_map(
        shards, mesh=mesh, in_specs=placed, out_specs=P("seq", "mp"), check_vma=False
    )
```

```python
import functools

import jax
import jax.numpy as jnp
from jax import lax
from jax.experimental import pallas as pl
from jax.experimental.pallas import tpu as pltpu
from jax.sharding import PartitionSpec as P

HEAD_DIM = 128
WINDOW = 1024
DOCS = 4
MP = 4
ROWS = 512
HALF = 256
FEATURES = 1344
STEP = 672
HEADS_LOCAL = 4
KV_WIDTH = 256
PAIR = 2 * KV_WIDTH
DOC_SHARDS = 8
HELD = 128
STRIP = FEATURES // 4
VMEM_LIMIT = 60 * 1024 * 1024

epsilon = 1e-06
query_scalar = 168.0
rope_base = 10000.0
F32 = jnp.float32
BF16 = jnp.bfloat16


def cost(flops, moved, exps=0):
    return pl.CostEstimate(flops=flops, bytes_accessed=moved, transcendentals=exps)


def params():
    return pltpu.CompilerParams(vmem_limit_bytes=VMEM_LIMIT)


def across_mp(array, flip):
    return lax.ppermute(array, "mp", [(i, i ^ flip) for i in range(MP)])


def seq_place(x, y_lo, z):
    return x * 8 + y_lo * 4 + z


def along_x(array, by):
    pairs = [
        (seq_place(x, y, z), seq_place((x + by) % 4, y, z))
        for x in range(4)
        for y in range(2)
        for z in range(4)
    ]
    return lax.ppermute(array, "seq", pairs)


def along_z(array, by):
    pairs = [
        (seq_place(x, y, z), seq_place(x, y, (z + by) % 4))
        for x in range(4)
        for y in range(2)
        for z in range(4)
    ]
    return lax.ppermute(array, "seq", pairs)


def to_twin(array):
    pairs = [(i, i ^ 4) for i in range(DOCS * DOC_SHARDS)]
    return lax.ppermute(array, "seq", pairs)


def z_flip(array, flip):
    return lax.ppermute(array, "seq", [(i, i ^ flip) for i in range(DOCS * DOC_SHARDS)])


def within_doc(array, by):
    pairs = [
        (d * DOC_SHARDS + i, d * DOC_SHARDS + (i + by) % DOC_SHARDS)
        for d in range(DOCS)
        for i in range(DOC_SHARDS)
    ]
    return lax.ppermute(array, "seq", pairs)


def after(array, *others):
    return lax.optimization_barrier((array, *others))[0]


TN = (((0,), (0,)), ((), ()))
NT = (((1,), (1,)), ((), ()))


IN_HBM = pl.BlockSpec(memory_space=pltpu.HBM)


def add_projection(x_ref, gain, wq, wk, wv, acc, squares):
    x = jnp.transpose(x_ref[...]).astype(F32)
    squares[...] += jnp.broadcast_to(jnp.sum(x * x, 1, keepdims=True), squares.shape)
    scaled = (x * gain[0]).astype(BF16)
    acc[:, :512] += jnp.dot(scaled, wq[...], preferred_element_type=F32)
    acc[:, 512:768] += jnp.dot(scaled, wk[...], preferred_element_type=F32)
    acc[:, 768:] += jnp.dot(scaled, wv[...], preferred_element_type=F32)


def first_kernel(order, x0, x1, gain, wq, wk, wv, acc, squares):
    step = pl.program_id(0)

    @pl.when(step == 0)
    def _():
        acc[...] = jnp.zeros_like(acc)
        squares[...] = jnp.zeros_like(squares)

    for number, x_ref in enumerate((x0, x1)):

        @pl.when(step // 2 == number)
        def _(x_ref=x_ref):
            add_projection(x_ref, gain, wq, wk, wv, acc, squares)


def last_kernel(
    order, x0, x1, gain, wq, wk, wv, gate, acc_in, squares_in, cosine, sine, q_ref, kv_ref, acc, squares
):
    step = pl.program_id(0)

    @pl.when(step == 0)
    def _():
        acc[...] = acc_in[...]
        squares[...] = squares_in[...]

    for number, x_ref in enumerate((x0, x1)):

        @pl.when(step // 2 == number)
        def _(x_ref=x_ref):
            add_projection(x_ref, gain, wq, wk, wv, acc, squares)

    @pl.when(step == 3)
    def _():
        scale = lax.rsqrt(squares[...] * (1.0 / (MP * FEATURES)) + epsilon)
        cos_all = cosine[...]
        sin_all = sine[...]
        for head in range(6):
            cols = slice(head * HEAD_DIM, (head + 1) * HEAD_DIM)
            part = acc[:, cols] * scale
            turned = part * cos_all + pltpu.roll(part, 64, 1) * sin_all
            if head < HEADS_LOCAL:
                q_ref[:, cols] = (turned * query_scalar ** (-0.5)).astype(BF16)
            else:
                at = (head - HEADS_LOCAL) * HEAD_DIM
                kv_ref[:, at : at + HEAD_DIM] = turned.astype(BF16)
        kv_ref[:, KV_WIDTH : KV_WIDTH + HEAD_DIM] = (acc[:, 768:896] * scale).astype(BF16)
        kv_ref[:, KV_WIDTH + HEAD_DIM :] = (acc[:, 896:] * scale).astype(BF16)


def chunk_specs(rows, first):
    chunk = lambda width: pl.BlockSpec(
        (STEP, width), lambda i, order: (order[first + i // 2] * 2 + i % 2, 0)
    )
    return [
        pl.BlockSpec((STEP, rows), lambda i, order: (jnp.minimum(i, 1), 0)),
        pl.BlockSpec((STEP, rows), lambda i, order: (jnp.maximum(i - 2, 0), 0)),
        pl.BlockSpec(
            (1, 1, STEP), lambda i, order: (order[first + i // 2] * 2 + i % 2, 0, 0)
        ),
        chunk(512),
        chunk(256),
        chunk(256),
    ]


def project_first(order, xs, gain, wq, wk, wv):
    full = lambda shape: pl.BlockSpec(shape, lambda i, order: (0,) * len(shape))
    shapes = [(ROWS, 1024), (ROWS, HEAD_DIM)]
    return pl.pallas_call(
        first_kernel,
        grid_spec=pltpu.PrefetchScalarGridSpec(
            num_scalar_prefetch=1,
            grid=(4,),
            in_specs=chunk_specs(ROWS, 0),
            out_specs=[full(s) for s in shapes],
        ),
        out_shape=[jax.ShapeDtypeStruct(s, F32) for s in shapes],
        compiler_params=params(),
        cost_estimate=cost(1, 1),
    )(order, *xs, gain, wq, wk, wv)


def project_last(half, order, xs, gain, wq, wk, wv, gate, carried, tables):
    place = lambda i, order: (half, 0)
    out = lambda i, order: (0, 0)
    return pl.pallas_call(
        last_kernel,
        grid_spec=pltpu.PrefetchScalarGridSpec(
            num_scalar_prefetch=1,
            grid=(4,),
            in_specs=chunk_specs(HALF, 2)
            + [
                IN_HBM,
                pl.BlockSpec((HALF, 1024), place),
                pl.BlockSpec((HALF, HEAD_DIM), place),
                pl.BlockSpec((HALF, HEAD_DIM), place),
                pl.BlockSpec((HALF, HEAD_DIM), place),
            ],
            out_specs=[pl.BlockSpec((HALF, 512), out)] * 2,
            scratch_shapes=[pltpu.VMEM((HALF, 1024), F32), pltpu.VMEM((HALF, HEAD_DIM), F32)],
        ),
        out_shape=[jax.ShapeDtypeStruct((HALF, 512), BF16)] * 2,
        compiler_params=params(),
        cost_estimate=cost(1, 1),
    )(order, *xs, gain, wq, wk, wv, gate, *carried, *tables)


def attention_kernel(half, where, ids, lengths, reals, q_ref, own_a, own_b, one_a, one_b, two_a, two_b, *refs):
    prefix, (out, held, sems) = refs[:4], refs[4:]
    local = where[2]
    length = lengths[ids[where[1]]]
    real = reals[where[1]]

    def copies(branch):
        late = [
            (prefix[r].at[1], pl.multiple_of((where[3] ^ r) * HELD, HELD), HELD) for r in range(4)
        ]
        early = [
            (prefix[r].at[0], pl.multiple_of((where[3] ^ r) * HELD, HELD), HELD) for r in range(4)
        ]
        one = [(one_a, ROWS, HALF), (one_b, ROWS + HALF, HALF)]
        two = [(two_a, 0, HALF), (two_b, HALF, HALF)]
        if branch == 0:
            got = early + [(a, pl.multiple_of(at + ROWS, HELD), n) for a, at, n in late]
        elif branch == 1:
            got = late + one
        else:
            got = two + one
        return [
            pltpu.make_async_copy(a, held.at[pl.ds(at, n)], sems.at[i])
            for i, (a, at, n) in enumerate(got)
        ]

    for branch in range(3):

        @pl.when(local == branch if branch < 2 else local >= 2)
        def _(branch=branch):
            started = copies(branch)
            for one in started:
                one.start()
            for one in started:
                one.wait()

    column = lax.broadcasted_iota(jnp.int32, (1, ROWS), 1)
    shift_two = jnp.where(local < 2, length, 0)
    limit_two = jnp.where(local < 2, WINDOW - ROWS * local - length, 0)
    shift_one = jnp.where(local < 1, length, 0)
    limit_one = jnp.where(local < 1, ROWS - length, 0)
    place_two = (column - shift_two) & (ROWS - 1)
    place_one = (column - shift_one) & (ROWS - 1)
    one_ok = place_one >= limit_one
    block = 128
    for chunk in range(HALF // block):
        start = chunk * block
        reach = start + block
        row = start + lax.broadcasted_iota(jnp.int32, (block, 1), 0)
        two_ok = place_two > jnp.maximum(row + half * HALF, limit_two - 1)
        own_ok = column[:, :reach] <= row
        row_real = row + half * HALF + local * ROWS < real
        for head in range(HEADS_LOCAL):
            k_cols = slice((head // 2) * HEAD_DIM, (head // 2 + 1) * HEAD_DIM)
            v_cols = slice(KV_WIDTH + k_cols.start, KV_WIDTH + k_cols.stop)
            cols = slice(head * HEAD_DIM, (head + 1) * HEAD_DIM)
            q = q_ref[start:reach, cols]
            parts = [
                (two_ok, held[:ROWS, k_cols], held[:ROWS, v_cols]),
                (one_ok, held[ROWS:, k_cols], held[ROWS:, v_cols]),
            ]
            if half:
                parts.append((None, own_a[:, k_cols], own_a[:, v_cols]))
            last = own_b if half else own_a
            parts.append((own_ok, last[:reach, k_cols], last[:reach, v_cols]))
            scores = []
            for ok, keys, _ in parts:
                s = lax.dot_general(q, keys, NT, preferred_element_type=F32)
                scores.append(s if ok is None else jnp.where(ok, s, -1e30))
            top = functools.reduce(
                jnp.maximum, [jnp.max(s, 1, keepdims=True) for s in scores]
            )
            total = 0.0
            got = 0.0
            for s, (_, _, values) in zip(scores, parts):
                weights = jnp.exp(s - top)
                total += jnp.sum(weights, 1, keepdims=True)
                got += jnp.dot(weights.astype(BF16), values, preferred_element_type=F32)
            got = jnp.where(row_real, got / total, 0.0)
            out[start:reach, cols] = got.astype(BF16)


def attention(half, scalars, q, own_a, own_b, one_a, one_b, two_a, two_b, prefix):
    full = pl.BlockSpec((HALF, 512), lambda i, *scalars: (0, 0))
    return pl.pallas_call(
        functools.partial(attention_kernel, half),
        grid_spec=pltpu.PrefetchScalarGridSpec(
            num_scalar_prefetch=4,
            grid=(1,),
            in_specs=[full] * 3 + [IN_HBM] * 8,
            out_specs=full,
            scratch_shapes=[
                pltpu.VMEM((2 * ROWS, PAIR), BF16),
                pltpu.SemaphoreType.DMA((8,)),
            ],
        ),
        out_shape=jax.ShapeDtypeStruct((HALF, 512), BF16),
        compiler_params=params(),
        cost_estimate=cost(
            4 * HEADS_LOCAL * HALF * 1536 * 128, 2_500_000, HEADS_LOCAL * HALF * 1536
        ),
    )(*scalars, q, own_a, own_b, one_a, one_b, two_a, two_b, *prefix)


def turn_kernel(where, w_ref, gate, own, near, piece_a, piece_b, turned):
    step = pl.program_id(0)
    strip = pl.ds(pl.multiple_of(where[3] * STRIP, 16), STRIP)
    for m in range(MP):
        columns = lambda flip: slice((m ^ flip) * FEATURES, ((m ^ flip) + 1) * FEATURES)

        @pl.when(where[0] == m)
        def _(columns=columns):
            own[...] = jnp.transpose(w_ref[:, columns(0)])
            near[...] = jnp.transpose(w_ref[:, columns(1)])

            @pl.when(step == where[1])
            def _():
                turned[...] = jnp.transpose(w_ref[:, columns(2)])
                piece_a[...] = turned[strip, :]
                turned[...] = jnp.transpose(w_ref[:, columns(3)])
                piece_b[...] = turned[strip, :]


def turned_weights(where, w_out, gate):
    whole = pl.BlockSpec((FEATURES, 128), lambda i, where: (0, i))
    piece = pl.BlockSpec((STRIP, 128), lambda i, where: (0, 0))
    return pl.pallas_call(
        turn_kernel,
        grid_spec=pltpu.PrefetchScalarGridSpec(
            num_scalar_prefetch=1,
            grid=(4,),
            in_specs=[pl.BlockSpec((128, MP * FEATURES), lambda i, where: (i, 0)), IN_HBM],
            out_specs=[whole, whole, piece, piece],
            scratch_shapes=[pltpu.VMEM((FEATURES, 128), BF16)],
        ),
        out_shape=[jax.ShapeDtypeStruct((FEATURES, 512), BF16)] * 2
        + [jax.ShapeDtypeStruct((STRIP, 128), BF16)] * 2,
        compiler_params=params(),
        cost_estimate=cost(1, 1),
    )(where, w_out, gate)


def pick_kernel(where, ids, lengths, rows_ref, gate, *outs):
    step = pl.program_id(0)
    reach = lengths[ids[(where[1] + step) & 3]]
    held_at = where[4] * HELD + lax.broadcasted_iota(jnp.int32, (HELD, 1), 0)
    wanted = (held_at < reach) & (held_at >= reach - WINDOW)
    for number, out in enumerate(outs):

        @pl.when(step == number)
        def _(out=out):
            for part in range(2):
                rows = rows_ref[0, :, part, :].astype(F32)
                out[:, part * KV_WIDTH : (part + 1) * KV_WIDTH] = jnp.where(
                    wanted, rows, 0.0
                ).astype(BF16)


def picked_rows(where, ids, lengths, prefix_cache, gate):
    return pl.pallas_call(
        pick_kernel,
        grid_spec=pltpu.PrefetchScalarGridSpec(
            num_scalar_prefetch=3,
            grid=(4,),
            in_specs=[
                pl.BlockSpec(
                    (1, HELD, 2, KV_WIDTH),
                    lambda i, where, ids, lengths: (ids[(where[1] + i) & 3], 0, 0, 0),
                ),
                IN_HBM,
            ],
            out_specs=[pl.BlockSpec((HELD, PAIR), lambda i, *scalars: (0, 0))] * 4,
        ),
        out_shape=[jax.ShapeDtypeStruct((HELD, PAIR), BF16)] * 4,
        compiler_params=params(),
        cost_estimate=cost(1, 1),
    )(where, ids, lengths, prefix_cache, gate)


def order_kernel(where, ids, lengths, mine, twin, out):
    length = lengths[ids[where[1]]]
    row = where[2] * HELD + lax.broadcasted_iota(jnp.int32, (HELD, 1), 0)
    late = ((row - length) & (WINDOW - 1)) >= ROWS
    a = mine[...].astype(F32)
    b = twin[...].astype(F32)
    out[0] = jnp.where(late, b, a).astype(BF16)
    out[1] = jnp.where(late, a, b).astype(BF16)


def ordered_rows(where, ids, lengths, mine, twin):
    part = pl.BlockSpec((HELD, PAIR), lambda i, *scalars: (0, 0))
    return pl.pallas_call(
        order_kernel,
        grid_spec=pltpu.PrefetchScalarGridSpec(
            num_scalar_prefetch=3,
            grid=(1,),
            in_specs=[part, part],
            out_specs=pl.BlockSpec((2, HELD, PAIR), lambda i, *scalars: (0, 0, 0)),
        ),
        out_shape=jax.ShapeDtypeStruct((2, HELD, PAIR), BF16),
        compiler_params=params(),
        cost_estimate=cost(1, 1),
    )(where, ids, lengths, mine, twin)


def near_kernel(c0a, c0b, c1a, c1b, w0, w1, out):
    for half, (c0, c1) in enumerate(((c0a, c1a), (c0b, c1b))):
        out[:, half * HALF : (half + 1) * HALF] = lax.dot_general(
            w0[...], c0[...], NT, preferred_element_type=F32
        ) + lax.dot_general(w1[...], c1[...], NT, preferred_element_type=F32)


def near_output(contexts, weights):
    full = lambda shape: pl.BlockSpec(shape, lambda i: (0, 0))
    strip = pl.BlockSpec((STRIP, 512), lambda i: (i, 0))
    return pl.pallas_call(
        near_kernel,
        grid=(4,),
        in_specs=[full((HALF, 512))] * 4 + [strip] * 2,
        out_specs=strip,
        out_shape=jax.ShapeDtypeStruct((FEATURES, ROWS), F32),
        compiler_params=params(),
        cost_estimate=cost(2 * ROWS * 1024 * FEATURES, 6_000_000),
    )(*contexts, *weights)


def far_kernel(where, c0a, c0b, c1a, c1b, near, p0, p1, p2, p3, out, squares, held, sems):
    z, x = where[3], where[1]
    pending = []
    for j, pieces in enumerate((p0, p1, p2, p3)):
        lanes = pl.multiple_of(((x - j) & 3) * HEAD_DIM, HEAD_DIM)
        for r in range(4):
            rows = pl.multiple_of(((z - r) & 3) * STRIP, 16)
            for b in range(2):
                copy = pltpu.make_async_copy(
                    pieces.at[r, b],
                    held.at[b, pl.ds(rows, STRIP), pl.ds(lanes, HEAD_DIM)],
                    sems.at[j * 8 + r * 2 + b],
                )
                copy.start()
                pending.append(copy)
    for copy in pending:
        copy.wait()
    for half, (c0, c1) in enumerate(((c0a, c1a), (c0b, c1b))):
        cols = slice(half * HALF, (half + 1) * HALF)
        total = jnp.zeros((1, HALF), F32)
        for strip in range(4):
            rows = slice(strip * STRIP, (strip + 1) * STRIP)
            got = (
                near[rows, cols]
                + lax.dot_general(held[0, rows], c0[...], NT, preferred_element_type=F32)
                + lax.dot_general(held[1, rows], c1[...], NT, preferred_element_type=F32)
            )
            out[rows, cols] = got
            total += jnp.sum(got * got, 0, keepdims=True)
        squares[:, cols] = total


def far_output(where, contexts, near, pieces):
    full = lambda shape: pl.BlockSpec(shape, lambda i, where: (0, 0))
    return pl.pallas_call(
        far_kernel,
        grid_spec=pltpu.PrefetchScalarGridSpec(
            num_scalar_prefetch=1,
            grid=(1,),
            in_specs=[full((HALF, 512))] * 4 + [full((FEATURES, ROWS))] + [IN_HBM] * 4,
            out_specs=[full((FEATURES, ROWS)), full((1, ROWS))],
            scratch_shapes=[
                pltpu.VMEM((2, FEATURES, 512), BF16),
                pltpu.SemaphoreType.DMA((32,)),
            ],
        ),
        out_shape=[
            jax.ShapeDtypeStruct((FEATURES, ROWS), F32),
            jax.ShapeDtypeStruct((1, ROWS), F32),
        ],
        compiler_params=params(),
        cost_estimate=cost(2 * ROWS * 1024 * FEATURES, 8_000_000),
    )(where, *contexts, near, *pieces)


def rope_tables(places):
    lane = jnp.arange(HEAD_DIM)
    frequency = rope_base ** (-((lane % 64).astype(F32) * 2.0 / HEAD_DIM))
    angles = places.astype(F32)[:, None] * frequency[None, :]
    return jnp.cos(angles), jnp.where(lane[None, :] < 64, -jnp.sin(angles), jnp.sin(angles))


def shards(
    tokens,
    gain_pre,
    w_query,
    w_key,
    w_value,
    w_out,
    gain_post,
    prefix_cache,
    template_ids,
    prefix_lengths,
    doc_lengths,
):
    member = lax.axis_index("mp")
    place = lax.axis_index("seq")
    doc = place // DOC_SHARDS
    local = place % DOC_SHARDS
    where = jnp.stack(
        [member, doc, local, place % 4, place, member, member ^ 1, member ^ 2, member ^ 3]
    ).astype(jnp.int32)
    scalars = (where, template_ids, prefix_lengths)

    turned_tokens = tokens.T
    near = across_mp(turned_tokens, 1)
    far_a = across_mp(turned_tokens[:, :HALF], 2)

    mine, *others = picked_rows(*scalars, prefix_cache, near)
    for by, other in enumerate(others, 1):
        mine = mine + along_x(other, by)
    ordered = ordered_rows(*scalars, mine, to_twin(mine))
    prefix = [ordered] + [z_flip(ordered, flip) for flip in (1, 2, 3)]

    template = jnp.sum(jnp.where(jnp.arange(DOCS) == doc, template_ids, 0))
    length = jnp.sum(jnp.where(jnp.arange(8) == template, prefix_lengths, 0))
    tables = rope_tables(length + local * ROWS + jnp.arange(ROWS))
    gain = gain_pre.reshape(2 * MP, 1, STEP)
    order = where[5:]
    weights = (w_query, w_key, w_value)
    carried = project_first(order, [turned_tokens, near], gain, *weights)
    far_b = across_mp(after(turned_tokens[:, HALF:], far_a, carried[1]), 2)

    w_own, w_give, piece_a, piece_b = turned_weights(where, w_out, carried[1])
    w_near = across_mp(w_give, 1)
    w_piece = jnp.stack([across_mp(piece_a, 2), across_mp(piece_b, 3)])
    w_line = jnp.stack([w_piece] + [along_z(w_piece, by) for by in (1, 2, 3)])
    w_far = [w_line] + [along_x(w_line, by) for by in (1, 2, 3)]

    gate = near
    q_parts, kv_parts, one_back, two_back = [], [], [], []
    for half, far in enumerate((far_a, far_b)):
        q, kv = project_last(
            half, order, [far, across_mp(far, 1)], gain, *weights, gate, carried, tables
        )
        gate = kv
        q_parts.append(q)
        kv_parts.append(kv)
        one_back.append(within_doc(kv, 1))
        two_back.append(within_doc(kv, 2))
    scalars = (*scalars, doc_lengths)
    c_own, c_near, c_far, c_far_near = [], [], [], []
    for half in range(2):
        context = attention(
            half, scalars, q_parts[half], *kv_parts, *one_back, *two_back, prefix
        )
        c_own.append(context)
        c_far.append(across_mp(context, 2))
        c_near.append(across_mp(context, 1))
        c_far_near.append(across_mp(c_far[-1], 1))
    near_sum = near_output([*c_own, *c_near], [w_own, w_near])
    attended, own_squares = far_output(where, [*c_far, *c_far_near], near_sum, w_far)
    total = own_squares
    for flip in (1, 2, 3):
        total = total + across_mp(own_squares, flip)
    scale = lax.rsqrt(total * (1.0 / (MP * FEATURES)) + epsilon)
    result = turned_tokens.astype(F32) + gain_post[:, None] * attended * scale
    return result.astype(BF16).T


def solution(mesh):
    placed = (
        P("seq", "mp"),
        P(),
        P(None, "mp"),
        P(None, "mp"),
        P(None, "mp"),
        P("mp", None),
        P("mp"),
        P(None, "seq", None, "mp"),
        P(),
        P(),
        P(),
    )
    return jax.shard_map(
        shards, mesh=mesh, in_specs=placed, out_specs=P("seq", "mp"), check_vma=False
    )
```

```python
import functools

import jax
import jax.numpy as jnp
from jax import lax
from jax.experimental import pallas as pl
from jax.experimental.pallas import tpu as pltpu
from jax.sharding import PartitionSpec as P

HEAD_DIM = 128
WINDOW = 1024
DOCS = 4
MP = 4
ROWS = 512
HALF = 256
FEATURES = 1344
STEP = 672
HEADS_LOCAL = 4
KV_WIDTH = 256
PAIR = 2 * KV_WIDTH
DOC_SHARDS = 8
HELD = 128
STRIP = FEATURES // 4
VMEM_LIMIT = 63 * 1024 * 1024

epsilon = 1e-06
query_scalar = 168.0
rope_base = 10000.0
F32 = jnp.float32
BF16 = jnp.bfloat16


def cost(flops, moved, exps=0):
    return pl.CostEstimate(flops=flops, bytes_accessed=moved, transcendentals=exps)


def params():
    return pltpu.CompilerParams(vmem_limit_bytes=VMEM_LIMIT)


def across_mp(array, flip):
    return lax.ppermute(array, "mp", [(i, i ^ flip) for i in range(MP)])


def seq_place(x, y_lo, z):
    return x * 8 + y_lo * 4 + z


def along_x(array, by):
    pairs = [
        (seq_place(x, y, z), seq_place((x + by) % 4, y, z))
        for x in range(4)
        for y in range(2)
        for z in range(4)
    ]
    return lax.ppermute(array, "seq", pairs)


def along_z(array, by):
    pairs = [
        (seq_place(x, y, z), seq_place(x, y, (z + by) % 4))
        for x in range(4)
        for y in range(2)
        for z in range(4)
    ]
    return lax.ppermute(array, "seq", pairs)


def to_twin(array):
    pairs = [(i, i ^ 4) for i in range(DOCS * DOC_SHARDS)]
    return lax.ppermute(array, "seq", pairs)


def z_flip(array, flip):
    return lax.ppermute(array, "seq", [(i, i ^ flip) for i in range(DOCS * DOC_SHARDS)])


def within_doc(array, by):
    pairs = [
        (d * DOC_SHARDS + i, d * DOC_SHARDS + (i + by) % DOC_SHARDS)
        for d in range(DOCS)
        for i in range(DOC_SHARDS)
    ]
    return lax.ppermute(array, "seq", pairs)


def after(array, *others):
    return lax.optimization_barrier((array, *others))[0]


TN = (((0,), (0,)), ((), ()))
NT = (((1,), (1,)), ((), ()))


IN_HBM = pl.BlockSpec(memory_space=pltpu.HBM)


def project_kernel(chunks, first, last, order, *refs):
    step = pl.program_id(0)
    xs, refs = refs[:chunks], refs[chunks:]
    gain, wq, wk, wv = refs[:4]
    if last:
        acc_in, squares_in, cosine, sine, q_ref, kv_ref, acc, squares = refs[-8:]
    elif first:
        acc, squares = refs[-2:]
    else:
        acc_in, squares_in, acc, squares = refs[-4:]

    for number in range(chunks):

        @pl.when(step // 2 == number)
        def _(number=number):
            x = jnp.transpose(xs[number][...]).astype(F32)
            scaled = (x * gain[0]).astype(BF16)
            parts = (
                jnp.dot(scaled, wq[...], preferred_element_type=F32),
                jnp.dot(scaled, wk[...], preferred_element_type=F32),
                jnp.dot(scaled, wv[...], preferred_element_type=F32),
                jnp.broadcast_to(jnp.sum(x * x, 1, keepdims=True), squares.shape),
            )

            def put(sources):
                at = 0
                for part, source in zip(parts[:3], sources):
                    cols = slice(at, at + part.shape[1])
                    acc[:, cols] = part if source is None else source[:, cols] + part
                    at = cols.stop
                squares[...] = parts[3] if sources[3] is None else sources[3][...] + parts[3]

            if number:
                put((acc, acc, acc, squares))
            else:

                @pl.when(step == 0)
                def _():
                    put((None,) * 4 if first else (acc_in, acc_in, acc_in, squares_in))

                @pl.when(step == 1)
                def _():
                    put((acc, acc, acc, squares))

    if last:

        @pl.when(step == 2 * chunks - 1)
        def _():
            scale = lax.rsqrt(squares[...] * (1.0 / (MP * FEATURES)) + epsilon)
            cos_all = cosine[...]
            sin_all = sine[...]
            for head in range(6):
                cols = slice(head * HEAD_DIM, (head + 1) * HEAD_DIM)
                part = acc[:, cols] * scale
                turned = part * cos_all + pltpu.roll(part, 64, 1) * sin_all
                if head < HEADS_LOCAL:
                    q_ref[:, cols] = (turned * query_scalar ** (-0.5)).astype(BF16)
                else:
                    at = (head - HEADS_LOCAL) * HEAD_DIM
                    kv_ref[:, at : at + HEAD_DIM] = turned.astype(BF16)
            for head in range(2):
                at = KV_WIDTH + head * HEAD_DIM
                part = acc[:, 768 + head * HEAD_DIM : 896 + head * HEAD_DIM] * scale
                kv_ref[:, at : at + HEAD_DIM] = part.astype(BF16)


def project(order, start, xs, gain, weights, gates=(), carried=(), tables=()):
    chunks = len(xs)
    full = lambda shape: pl.BlockSpec(shape, lambda i, order: (0,) * len(shape))
    at = lambda i, order: order[5 + start + i // 2] * 2 + i % 2
    acc_shapes = [(ROWS, 1024), (ROWS, HEAD_DIM)]
    if tables:
        out_shape = [jax.ShapeDtypeStruct((ROWS, 512), BF16)] * 2
        scratch = [pltpu.VMEM(shape, F32) for shape in acc_shapes]
    else:
        out_shape = [jax.ShapeDtypeStruct(shape, F32) for shape in acc_shapes]
        scratch = []
    return pl.pallas_call(
        functools.partial(project_kernel, chunks, not carried, bool(tables)),
        grid_spec=pltpu.PrefetchScalarGridSpec(
            num_scalar_prefetch=1,
            grid=(2 * chunks,),
            in_specs=[
                pl.BlockSpec((STEP, ROWS), lambda i, order, k=k: (jnp.clip(i - 2 * k, 0, 1), 0))
                for k in range(chunks)
            ]
            + [pl.BlockSpec((1, 1, STEP), lambda i, order: (at(i, order), 0, 0))]
            + [
                pl.BlockSpec((STEP, width), lambda i, order: (at(i, order), 0))
                for width in (512, 256, 256)
            ]
            + [IN_HBM] * len(gates)
            + [full(one.shape) for one in (*carried, *tables)],
            out_specs=[full(one.shape) for one in out_shape],
            scratch_shapes=scratch,
        ),
        out_shape=out_shape,
        compiler_params=params(),
        cost_estimate=cost(6_000_000_000, 20_000_000) if tables else cost(1, 1),
    )(order, *xs, gain, *weights, *gates, *carried, *tables)


def attention_kernel(where, ids, lengths, reals, q_ref, own, one_back, two_back, *refs):
    prefix, twin, _, _, _, out, held, lines, sems = refs
    local = where[2]
    length = lengths[ids[where[1]]]
    real = reals[where[1]]

    def fetch(pairs):
        copies = [pltpu.make_async_copy(a, b, sems.at[i]) for i, (a, b) in enumerate(pairs)]
        for one in copies:
            one.start()
        for one in copies:
            one.wait()

    def fetch_prefix():
        fetch(
            [
                (
                    source.at[r],
                    lines.at[side, pl.ds(pl.multiple_of((where[3] ^ r) * HELD, HELD), HELD)],
                )
                for side, source in enumerate((prefix, twin))
                for r in range(4)
            ]
        )

    def picked(late_part):
        row = lax.broadcasted_iota(jnp.int32, (ROWS, 1), 0)
        late = ((row - length) & (WINDOW - 1)) >= ROWS
        low = lines[0].astype(F32)
        high = lines[1].astype(F32)
        return (jnp.where(late, low, high) if late_part else jnp.where(late, high, low)).astype(
            BF16
        )

    @pl.when(local == 0)
    def _():
        fetch_prefix()
        held[:ROWS] = picked(False)
        held[ROWS:] = picked(True)

    @pl.when(local == 1)
    def _():
        fetch_prefix()
        held[:ROWS] = picked(True)
        fetch([(one_back, held.at[pl.ds(ROWS, ROWS)])])

    @pl.when(local >= 2)
    def _():
        fetch([(two_back, held.at[pl.ds(0, ROWS)]), (one_back, held.at[pl.ds(ROWS, ROWS)])])

    column = lax.broadcasted_iota(jnp.int32, (1, ROWS), 1)
    shift_two = jnp.where(local < 2, length, 0)
    limit_two = jnp.where(local < 2, WINDOW - ROWS * local - length, 0)
    shift_one = jnp.where(local < 1, length, 0)
    limit_one = jnp.where(local < 1, ROWS - length, 0)
    place_two = (column - shift_two) & (ROWS - 1)
    place_one = (column - shift_one) & (ROWS - 1)
    one_ok = place_one >= limit_one
    for half in range(2):
        mine = slice(half * HALF, (half + 1) * HALF)
        row = half * HALF + (lax.broadcasted_iota(jnp.int32, (2 * HALF, 1), 0) & (HALF - 1))
        two_ok = place_two > jnp.maximum(row, limit_two - 1)
        own_ok = column[:, mine] <= row
        row_real = row + local * ROWS < real
        for head in range(2):
            k_cols = slice(head * HEAD_DIM, (head + 1) * HEAD_DIM)
            v_cols = slice(KV_WIDTH + k_cols.start, KV_WIDTH + k_cols.stop)
            firsts = [(2 * head + i) * HEAD_DIM for i in range(2)]
            q = jnp.concatenate([q_ref[mine, at : at + HEAD_DIM] for at in firsts], 0)
            parts = [
                (two_ok, held[:ROWS, k_cols], held[:ROWS, v_cols]),
                (one_ok, held[ROWS:, k_cols], held[ROWS:, v_cols]),
            ]
            if half:
                parts.append((None, own[:HALF, k_cols], own[:HALF, v_cols]))
            parts.append((own_ok, own[mine, k_cols], own[mine, v_cols]))
            scores = []
            for ok, keys, _ in parts:
                s = lax.dot_general(q, keys, NT, preferred_element_type=F32)
                scores.append(s if ok is None else jnp.where(ok, s, -1e30))
            top = functools.reduce(jnp.maximum, [jnp.max(s, 1, keepdims=True) for s in scores])
            total = 0.0
            got = 0.0
            for s, (_, _, values) in zip(scores, parts):
                weights = jnp.exp(s - top)
                total += jnp.sum(weights, 1, keepdims=True)
                got += jnp.dot(weights.astype(BF16), values, preferred_element_type=F32)
            got = jnp.where(row_real, got / total, 0.0).astype(BF16)
            for i, at in enumerate(firsts):
                out[mine, at : at + HEAD_DIM] = got[i * HALF : (i + 1) * HALF]


def attention(scalars, q, own, one_back, two_back, prefix, gates):
    full = pl.BlockSpec((ROWS, 512), lambda i, *scalars: (0, 0))
    return pl.pallas_call(
        attention_kernel,
        grid_spec=pltpu.PrefetchScalarGridSpec(
            num_scalar_prefetch=4,
            grid=(1,),
            in_specs=[full] * 2 + [IN_HBM] * 7,
            out_specs=full,
            scratch_shapes=[
                pltpu.VMEM((2 * ROWS, PAIR), BF16),
                pltpu.VMEM((2, ROWS, PAIR), BF16),
                pltpu.SemaphoreType.DMA((8,)),
            ],
        ),
        out_shape=jax.ShapeDtypeStruct((ROWS, 512), BF16),
        compiler_params=params(),
        cost_estimate=cost(1, 1),
    )(*scalars, q, own, one_back, two_back, *prefix, *gates)


def piece_kernel(where, w_ref, gate, piece_a, piece_b, turned):
    strip = pl.ds(pl.multiple_of(where[3] * STRIP, 16), STRIP)
    for m in range(MP):

        @pl.when(where[0] == m)
        def _(m=m):
            for flip, piece in ((2, piece_a), (3, piece_b)):
                at = (m ^ flip) * FEATURES
                turned[...] = jnp.transpose(w_ref[:, at : at + FEATURES])
                piece[...] = turned[strip, :]


def turned_pieces(where, w_out, gate):
    piece = pl.BlockSpec((STRIP, 128), lambda i, where: (0, 0))
    return pl.pallas_call(
        piece_kernel,
        grid_spec=pltpu.PrefetchScalarGridSpec(
            num_scalar_prefetch=1,
            grid=(1,),
            in_specs=[pl.BlockSpec((128, MP * FEATURES), lambda i, where: (where[1], 0)), IN_HBM],
            out_specs=[piece, piece],
            scratch_shapes=[pltpu.VMEM((FEATURES, 128), BF16)],
        ),
        out_shape=[jax.ShapeDtypeStruct((STRIP, 128), BF16)] * 2,
        compiler_params=params(),
        cost_estimate=cost(1, 1),
    )(where, w_out, gate)


def turn_kernel(where, w_ref, gate, own, near):
    for m in range(MP):

        @pl.when(where[0] == m)
        def _(m=m):
            for flip, out in ((0, own), (1, near)):
                at = (m ^ flip) * FEATURES
                out[...] = jnp.transpose(w_ref[:, at : at + FEATURES])


def turned_weights(where, w_out, gate):
    whole = pl.BlockSpec((FEATURES, 128), lambda i, where: (0, i))
    return pl.pallas_call(
        turn_kernel,
        grid_spec=pltpu.PrefetchScalarGridSpec(
            num_scalar_prefetch=1,
            grid=(4,),
            in_specs=[pl.BlockSpec((128, MP * FEATURES), lambda i, where: (i, 0)), IN_HBM],
            out_specs=[whole, whole],
        ),
        out_shape=[jax.ShapeDtypeStruct((FEATURES, 512), BF16)] * 2,
        compiler_params=params(),
        cost_estimate=cost(1, 1),
    )(where, w_out, gate)


def pick_kernel(where, ids, lengths, rows_ref, gate, places, *outs):
    step = pl.program_id(0)

    @pl.when(step == 0)
    def _():
        first = lengths[ids[where[1]]] + where[2] * ROWS
        row = lax.broadcasted_iota(jnp.int32, (ROWS, HEAD_DIM), 0)
        places[...] = (row + first).astype(F32)

    reach = lengths[ids[(where[1] + step) & 3]]
    held_at = where[4] * HELD + lax.broadcasted_iota(jnp.int32, (HELD, 1), 0)
    wanted = (held_at < reach) & (held_at >= reach - WINDOW)
    for number, out in enumerate(outs):

        @pl.when(step == number)
        def _(out=out):
            for part in range(2):
                rows = rows_ref[0, :, part, :].astype(F32)
                out[:, part * KV_WIDTH : (part + 1) * KV_WIDTH] = jnp.where(
                    wanted, rows, 0.0
                ).astype(BF16)


def picked_rows(where, ids, lengths, prefix_cache, gate):
    return pl.pallas_call(
        pick_kernel,
        grid_spec=pltpu.PrefetchScalarGridSpec(
            num_scalar_prefetch=3,
            grid=(4,),
            in_specs=[
                pl.BlockSpec(
                    (1, HELD, 2, KV_WIDTH),
                    lambda i, where, ids, lengths: (ids[(where[1] + i) & 3], 0, 0, 0),
                ),
                IN_HBM,
            ],
            out_specs=[pl.BlockSpec((ROWS, HEAD_DIM), lambda i, *scalars: (0, 0))]
            + [pl.BlockSpec((HELD, PAIR), lambda i, *scalars: (0, 0))] * 4,
        ),
        out_shape=[jax.ShapeDtypeStruct((ROWS, HEAD_DIM), F32)]
        + [jax.ShapeDtypeStruct((HELD, PAIR), BF16)] * 4,
        compiler_params=params(),
        cost_estimate=cost(1, 1),
    )(where, ids, lengths, prefix_cache, gate)


def near_kernel(c0, c1, w0, w1, out):
    out[...] = lax.dot_general(
        w0[...], c0[...], NT, preferred_element_type=F32
    ) + lax.dot_general(w1[...], c1[...], NT, preferred_element_type=F32)


def near_output(contexts, weights):
    full = lambda shape: pl.BlockSpec(shape, lambda i: (0, 0))
    strip = pl.BlockSpec((STRIP, 512), lambda i: (i, 0))
    return pl.pallas_call(
        near_kernel,
        grid=(4,),
        in_specs=[full((ROWS, 512))] * 2 + [strip] * 2,
        out_specs=strip,
        out_shape=jax.ShapeDtypeStruct((FEATURES, ROWS), F32),
        compiler_params=params(),
        cost_estimate=cost(1, 1),
    )(*contexts, *weights)


def far_kernel(where, c0, c1, near, p0, p1, p2, p3, out, squares, held):
    step = pl.program_id(0)

    @pl.when(step == 0)
    def _():
        squares[...] = jnp.zeros_like(squares)

    for j, piece in enumerate((p0, p1, p2, p3)):
        lanes = pl.multiple_of(((where[1] - j) & 3) * HEAD_DIM, HEAD_DIM)
        for b in range(2):
            held[b, :, pl.ds(lanes, HEAD_DIM)] = piece[0, b]
    got = (
        near[...]
        + lax.dot_general(held[0], c0[...], NT, preferred_element_type=F32)
        + lax.dot_general(held[1], c1[...], NT, preferred_element_type=F32)
    )
    out[...] = got
    squares[...] += jnp.sum(got * got, 0, keepdims=True)


def far_output(where, contexts, near, pieces):
    full = lambda shape: pl.BlockSpec(shape, lambda i, where: (0, 0))
    strip = pl.BlockSpec((STRIP, ROWS), lambda i, where: (i, 0))
    piece = pl.BlockSpec(
        (1, 2, STRIP, HEAD_DIM), lambda i, where: ((where[3] - i) & 3, 0, 0, 0)
    )
    return pl.pallas_call(
        far_kernel,
        grid_spec=pltpu.PrefetchScalarGridSpec(
            num_scalar_prefetch=1,
            grid=(4,),
            in_specs=[full((ROWS, 512))] * 2 + [strip] + [piece] * 4,
            out_specs=[strip, full((1, ROWS))],
            scratch_shapes=[pltpu.VMEM((2, STRIP, 512), BF16)],
        ),
        out_shape=[
            jax.ShapeDtypeStruct((FEATURES, ROWS), F32),
            jax.ShapeDtypeStruct((1, ROWS), F32),
        ],
        compiler_params=params(),
        cost_estimate=cost(2 * ROWS * 1024 * FEATURES, 8_000_000),
    )(where, *contexts, near, *pieces)


def rope_tables(places):
    lane = jnp.arange(HEAD_DIM)
    frequency = rope_base ** (-((lane % 64).astype(F32) * 2.0 / HEAD_DIM))
    angles = places * frequency[None, :]
    return jnp.cos(angles), jnp.where(lane[None, :] < 64, -jnp.sin(angles), jnp.sin(angles))


def shards(
    tokens,
    gain_pre,
    w_query,
    w_key,
    w_value,
    w_out,
    gain_post,
    prefix_cache,
    template_ids,
    prefix_lengths,
    doc_lengths,
):
    member = lax.axis_index("mp")
    place = lax.axis_index("seq")
    doc = place // DOC_SHARDS
    local = place % DOC_SHARDS
    where = jnp.stack(
        [member, doc, local, place % 4, place, member, member ^ 1, member ^ 2, member ^ 3]
    ).astype(jnp.int32)
    scalars = (where, template_ids, prefix_lengths)

    turned_tokens = tokens.T
    near = across_mp(turned_tokens, 1)
    far = across_mp(turned_tokens, 2)

    places, mine, *others = picked_rows(*scalars, prefix_cache, near)
    for by, other in enumerate(others, 1):
        mine = mine + along_x(other, by)
    prefix = jnp.stack([mine] + [z_flip(mine, flip) for flip in (1, 2, 3)])
    tables = rope_tables(places)

    piece_a, piece_b = turned_pieces(where, w_out, others[0])
    crossed = (across_mp(piece_a, 2), across_mp(piece_b, 3))

    gain = gain_pre.reshape(2 * MP, 1, STEP)
    weights = (w_query, w_key, w_value)
    carried = project(where, 0, [turned_tokens, near], gain, weights, (piece_a,))
    far, piece_a, piece_b, prefix, *_ = lax.optimization_barrier(
        (far, *crossed, prefix, *carried, *tables)
    )
    w_piece = jnp.stack([piece_a, piece_b])
    prefix_twin = to_twin(prefix)
    queries, own = project(
        where, 2, [far, across_mp(far, 1)], gain, weights, (), carried, tables
    )
    w_parts = [w_piece] + [along_z(w_piece, by) for by in (1, 2, 3)]
    sent, *w_parts = lax.optimization_barrier((own, *w_parts, prefix_twin))[:5]
    one_back = within_doc(sent, 1)
    two_back = within_doc(sent, 2)
    w_line = jnp.stack(w_parts)
    w_next = along_x(w_line, 1)
    w_far = [w_line, w_next, along_x(w_next, 1), along_x(w_line, 3)]
    w_own, w_give = turned_weights(where, w_out, w_line)
    w_near = across_mp(w_give, 1)
    context = attention(
        (*scalars, doc_lengths), queries, own, one_back, two_back, (prefix, prefix_twin), (w_give, w_far[1], w_far[3])
    )
    c_far = across_mp(context, 2)
    c_near = across_mp(context, 1)
    near_sum = near_output([context, c_near], [w_own, w_near])
    attended, own_squares = far_output(where, [c_far, across_mp(c_far, 1)], near_sum, w_far)
    total = own_squares
    for flip in (1, 2, 3):
        total = total + across_mp(own_squares, flip)
    scale = lax.rsqrt(total * (1.0 / (MP * FEATURES)) + epsilon)
    result = turned_tokens.astype(F32) + gain_post[:, None] * attended * scale
    return result.astype(BF16).T


def solution(mesh):
    placed = (
        P("seq", "mp"),
        P(),
        P(None, "mp"),
        P(None, "mp"),
        P(None, "mp"),
        P("mp", None),
        P("mp"),
        P(None, "seq", None, "mp"),
        P(),
        P(),
        P(),
    )
    return jax.shard_map(
        shards, mesh=mesh, in_specs=placed, out_specs=P("seq", "mp"), check_vma=False
    )
```

```python
import functools

import jax
import jax.numpy as jnp
from jax import lax
from jax.experimental import pallas as pl
from jax.experimental.pallas import tpu as pltpu
from jax.sharding import PartitionSpec as P

HEAD_DIM = 128
WINDOW = 1024
DOCS = 4
MP = 4
ROWS = 512
HALF = 256
FEATURES = 1344
STEP = 672
HEADS_LOCAL = 4
KV_WIDTH = 256
PAIR = 2 * KV_WIDTH
DOC_SHARDS = 8
HELD = 128
STRIP = FEATURES // 4
VMEM_LIMIT = 63 * 1024 * 1024

epsilon = 1e-06
query_scalar = 168.0
rope_base = 10000.0
F32 = jnp.float32
BF16 = jnp.bfloat16


def cost(flops, moved, exps=0):
    return pl.CostEstimate(flops=flops, bytes_accessed=moved, transcendentals=exps)


def params():
    return pltpu.CompilerParams(vmem_limit_bytes=VMEM_LIMIT)


def across_mp(array, flip):
    return lax.ppermute(array, "mp", [(i, i ^ flip) for i in range(MP)])


def seq_place(x, y_lo, z):
    return x * 8 + y_lo * 4 + z


def along_x(array, by):
    pairs = [
        (seq_place(x, y, z), seq_place((x + by) % 4, y, z))
        for x in range(4)
        for y in range(2)
        for z in range(4)
    ]
    return lax.ppermute(array, "seq", pairs)


def along_z(array, by):
    pairs = [
        (seq_place(x, y, z), seq_place(x, y, (z + by) % 4))
        for x in range(4)
        for y in range(2)
        for z in range(4)
    ]
    return lax.ppermute(array, "seq", pairs)


def to_twin(array):
    pairs = [(i, i ^ 4) for i in range(DOCS * DOC_SHARDS)]
    return lax.ppermute(array, "seq", pairs)


def z_flip(array, flip):
    return lax.ppermute(array, "seq", [(i, i ^ flip) for i in range(DOCS * DOC_SHARDS)])


def within_doc(array, by):
    pairs = [
        (d * DOC_SHARDS + i, d * DOC_SHARDS + (i + by) % DOC_SHARDS)
        for d in range(DOCS)
        for i in range(DOC_SHARDS)
    ]
    return lax.ppermute(array, "seq", pairs)


def after(array, *others):
    return lax.optimization_barrier((array, *others))[0]


TN = (((0,), (0,)), ((), ()))
NT = (((1,), (1,)), ((), ()))


IN_HBM = pl.BlockSpec(memory_space=pltpu.HBM)


def project_kernel(chunks, first, last, order, *refs):
    step = pl.program_id(0)
    xs, refs = refs[:chunks], refs[chunks:]
    gain, wq, wk, wv = refs[:4]
    if last:
        acc_in, squares_in, cosine, sine, q_ref, kv_ref, acc, squares = refs[-8:]
    elif first:
        acc, squares = refs[-2:]
    else:
        acc_in, squares_in, acc, squares = refs[-4:]

    for number in range(chunks):

        @pl.when(step // 2 == number)
        def _(number=number):
            x = jnp.transpose(xs[number][...]).astype(F32)
            scaled = (x * gain[0]).astype(BF16)
            parts = (
                jnp.dot(scaled, wq[...], preferred_element_type=F32),
                jnp.dot(scaled, wk[...], preferred_element_type=F32),
                jnp.dot(scaled, wv[...], preferred_element_type=F32),
                jnp.broadcast_to(jnp.sum(x * x, 1, keepdims=True), squares.shape),
            )

            def put(sources):
                at = 0
                for part, source in zip(parts[:3], sources):
                    cols = slice(at, at + part.shape[1])
                    acc[:, cols] = part if source is None else source[:, cols] + part
                    at = cols.stop
                squares[...] = parts[3] if sources[3] is None else sources[3][...] + parts[3]

            if number:
                put((acc, acc, acc, squares))
            else:

                @pl.when(step == 0)
                def _():
                    put((None,) * 4 if first else (acc_in, acc_in, acc_in, squares_in))

                @pl.when(step == 1)
                def _():
                    put((acc, acc, acc, squares))

    if last:

        @pl.when(step == 2 * chunks - 1)
        def _():
            scale = lax.rsqrt(squares[...] * (1.0 / (MP * FEATURES)) + epsilon)
            cos_all = cosine[...]
            sin_all = sine[...]
            for head in range(6):
                cols = slice(head * HEAD_DIM, (head + 1) * HEAD_DIM)
                part = acc[:, cols] * scale
                turned = part * cos_all + pltpu.roll(part, 64, 1) * sin_all
                if head < HEADS_LOCAL:
                    q_ref[:, cols] = (turned * query_scalar ** (-0.5)).astype(BF16)
                else:
                    at = (head - HEADS_LOCAL) * HEAD_DIM
                    kv_ref[:, at : at + HEAD_DIM] = turned.astype(BF16)
            for head in range(2):
                at = KV_WIDTH + head * HEAD_DIM
                part = acc[:, 768 + head * HEAD_DIM : 896 + head * HEAD_DIM] * scale
                kv_ref[:, at : at + HEAD_DIM] = part.astype(BF16)


def project(order, start, xs, gain, weights, gates=(), carried=(), tables=()):
    chunks = len(xs)
    full = lambda shape: pl.BlockSpec(shape, lambda i, order: (0,) * len(shape))
    at = lambda i, order: order[5 + start + i // 2] * 2 + i % 2
    acc_shapes = [(ROWS, 1024), (ROWS, HEAD_DIM)]
    if tables:
        out_shape = [jax.ShapeDtypeStruct((ROWS, 512), BF16)] * 2
        scratch = [pltpu.VMEM(shape, F32) for shape in acc_shapes]
    else:
        out_shape = [jax.ShapeDtypeStruct(shape, F32) for shape in acc_shapes]
        scratch = []
    return pl.pallas_call(
        functools.partial(project_kernel, chunks, not carried, bool(tables)),
        grid_spec=pltpu.PrefetchScalarGridSpec(
            num_scalar_prefetch=1,
            grid=(2 * chunks,),
            in_specs=[
                pl.BlockSpec((STEP, ROWS), lambda i, order, k=k: (jnp.clip(i - 2 * k, 0, 1), 0))
                for k in range(chunks)
            ]
            + [pl.BlockSpec((1, 1, STEP), lambda i, order: (at(i, order), 0, 0))]
            + [
                pl.BlockSpec((STEP, width), lambda i, order: (at(i, order), 0))
                for width in (512, 256, 256)
            ]
            + [IN_HBM] * len(gates)
            + [full(one.shape) for one in (*carried, *tables)],
            out_specs=[full(one.shape) for one in out_shape],
            scratch_shapes=scratch,
        ),
        out_shape=out_shape,
        compiler_params=params(),
        cost_estimate=cost(6_000_000_000, 20_000_000) if tables else cost(1, 1),
    )(order, *xs, gain, *weights, *gates, *carried, *tables)


def attention_kernel(where, ids, lengths, reals, q_ref, own, one_back, two_back, *refs):
    prefix, twin, _, out, held, lines, sems = refs
    local = where[2]
    length = lengths[ids[where[1]]]
    real = reals[where[1]]

    def fetch(pairs):
        copies = [pltpu.make_async_copy(a, b, sems.at[i]) for i, (a, b) in enumerate(pairs)]
        for one in copies:
            one.start()
        for one in copies:
            one.wait()

    def fetch_prefix():
        fetch(
            [
                (
                    source.at[r],
                    lines.at[side, pl.ds(pl.multiple_of((where[3] ^ r) * HELD, HELD), HELD)],
                )
                for side, source in enumerate((prefix, twin))
                for r in range(4)
            ]
        )

    def picked(late_part):
        row = lax.broadcasted_iota(jnp.int32, (ROWS, 1), 0)
        late = ((row - length) & (WINDOW - 1)) >= ROWS
        low = lines[0].astype(F32)
        high = lines[1].astype(F32)
        return (jnp.where(late, low, high) if late_part else jnp.where(late, high, low)).astype(
            BF16
        )

    @pl.when(local == 0)
    def _():
        fetch_prefix()
        held[:ROWS] = picked(False)
        held[ROWS:] = picked(True)

    @pl.when(local == 1)
    def _():
        fetch_prefix()
        held[:ROWS] = picked(True)
        fetch([(one_back, held.at[pl.ds(ROWS, ROWS)])])

    @pl.when(local >= 2)
    def _():
        fetch([(two_back, held.at[pl.ds(0, ROWS)]), (one_back, held.at[pl.ds(ROWS, ROWS)])])

    column = lax.broadcasted_iota(jnp.int32, (1, ROWS), 1)
    shift_two = jnp.where(local < 2, length, 0)
    limit_two = jnp.where(local < 2, WINDOW - ROWS * local - length, 0)
    shift_one = jnp.where(local < 1, length, 0)
    limit_one = jnp.where(local < 1, ROWS - length, 0)
    place_two = (column - shift_two) & (ROWS - 1)
    place_one = (column - shift_one) & (ROWS - 1)
    one_ok = place_one >= limit_one
    for half in range(2):
        mine = slice(half * HALF, (half + 1) * HALF)
        row = half * HALF + (lax.broadcasted_iota(jnp.int32, (2 * HALF, 1), 0) & (HALF - 1))
        two_ok = place_two > jnp.maximum(row, limit_two - 1)
        own_ok = column[:, mine] <= row
        row_real = row + local * ROWS < real
        for head in range(2):
            k_cols = slice(head * HEAD_DIM, (head + 1) * HEAD_DIM)
            v_cols = slice(KV_WIDTH + k_cols.start, KV_WIDTH + k_cols.stop)
            firsts = [(2 * head + i) * HEAD_DIM for i in range(2)]
            q = jnp.concatenate([q_ref[mine, at : at + HEAD_DIM] for at in firsts], 0)
            parts = [
                (two_ok, held[:ROWS, k_cols], held[:ROWS, v_cols]),
                (one_ok, held[ROWS:, k_cols], held[ROWS:, v_cols]),
            ]
            if half:
                parts.append((None, own[:HALF, k_cols], own[:HALF, v_cols]))
            parts.append((own_ok, own[mine, k_cols], own[mine, v_cols]))
            scores = []
            for ok, keys, _ in parts:
                s = lax.dot_general(q, keys, NT, preferred_element_type=F32)
                scores.append(s if ok is None else jnp.where(ok, s, -1e30))
            top = functools.reduce(jnp.maximum, [jnp.max(s, 1, keepdims=True) for s in scores])
            total = 0.0
            got = 0.0
            for s, (_, _, values) in zip(scores, parts):
                weights = jnp.exp(s - top)
                total += jnp.sum(weights, 1, keepdims=True)
                got += jnp.dot(weights.astype(BF16), values, preferred_element_type=F32)
            got = jnp.where(row_real, got / total, 0.0).astype(BF16)
            for i, at in enumerate(firsts):
                out[mine, at : at + HEAD_DIM] = got[i * HALF : (i + 1) * HALF]


def attention(scalars, q, own, one_back, two_back, prefix, gates):
    full = pl.BlockSpec((ROWS, 512), lambda i, *scalars: (0, 0))
    return pl.pallas_call(
        attention_kernel,
        grid_spec=pltpu.PrefetchScalarGridSpec(
            num_scalar_prefetch=4,
            grid=(1,),
            in_specs=[full] * 2 + [IN_HBM] * 5,
            out_specs=full,
            scratch_shapes=[
                pltpu.VMEM((2 * ROWS, PAIR), BF16),
                pltpu.VMEM((2, ROWS, PAIR), BF16),
                pltpu.SemaphoreType.DMA((8,)),
            ],
        ),
        out_shape=jax.ShapeDtypeStruct((ROWS, 512), BF16),
        compiler_params=params(),
        cost_estimate=cost(1, 1),
    )(*scalars, q, own, one_back, two_back, *prefix, *gates)


def piece_kernel(where, w_ref, gate, piece_a, piece_b, turned):
    strip = pl.ds(pl.multiple_of(where[3] * STRIP, 16), STRIP)
    for m in range(MP):

        @pl.when(where[0] == m)
        def _(m=m):
            for flip, piece in ((2, piece_a), (3, piece_b)):
                at = (m ^ flip) * FEATURES
                turned[...] = jnp.transpose(w_ref[:, at : at + FEATURES])
                piece[...] = turned[strip, :]


def turned_pieces(where, w_out, gate):
    piece = pl.BlockSpec((STRIP, 128), lambda i, where: (0, 0))
    return pl.pallas_call(
        piece_kernel,
        grid_spec=pltpu.PrefetchScalarGridSpec(
            num_scalar_prefetch=1,
            grid=(1,),
            in_specs=[pl.BlockSpec((128, MP * FEATURES), lambda i, where: (where[1], 0)), IN_HBM],
            out_specs=[piece, piece],
            scratch_shapes=[pltpu.VMEM((FEATURES, 128), BF16)],
        ),
        out_shape=[jax.ShapeDtypeStruct((STRIP, 128), BF16)] * 2,
        compiler_params=params(),
        cost_estimate=cost(1, 1),
    )(where, w_out, gate)


def turn_kernel(where, w_ref, gate, own, near):
    for m in range(MP):

        @pl.when(where[0] == m)
        def _(m=m):
            for flip, out in ((0, own), (1, near)):
                at = (m ^ flip) * FEATURES
                out[...] = jnp.transpose(w_ref[:, at : at + FEATURES])


def turned_weights(where, w_out, gate):
    whole = pl.BlockSpec((FEATURES, 128), lambda i, where: (0, i))
    return pl.pallas_call(
        turn_kernel,
        grid_spec=pltpu.PrefetchScalarGridSpec(
            num_scalar_prefetch=1,
            grid=(4,),
            in_specs=[pl.BlockSpec((128, MP * FEATURES), lambda i, where: (i, 0)), IN_HBM],
            out_specs=[whole, whole],
        ),
        out_shape=[jax.ShapeDtypeStruct((FEATURES, 512), BF16)] * 2,
        compiler_params=params(),
        cost_estimate=cost(1, 1),
    )(where, w_out, gate)


def pick_kernel(where, ids, lengths, rows_ref, gate, places, *outs):
    step = pl.program_id(0)

    @pl.when(step == 0)
    def _():
        first = lengths[ids[where[1]]] + where[2] * ROWS
        row = lax.broadcasted_iota(jnp.int32, (ROWS, HEAD_DIM), 0)
        places[...] = (row + first).astype(F32)

    reach = lengths[ids[(where[1] + step) & 3]]
    held_at = where[4] * HELD + lax.broadcasted_iota(jnp.int32, (HELD, 1), 0)
    wanted = (held_at < reach) & (held_at >= reach - WINDOW)
    for number, out in enumerate(outs):

        @pl.when(step == number)
        def _(out=out):
            for part in range(2):
                rows = rows_ref[0, :, part, :].astype(F32)
                out[:, part * KV_WIDTH : (part + 1) * KV_WIDTH] = jnp.where(
                    wanted, rows, 0.0
                ).astype(BF16)


def picked_rows(where, ids, lengths, prefix_cache, gate):
    return pl.pallas_call(
        pick_kernel,
        grid_spec=pltpu.PrefetchScalarGridSpec(
            num_scalar_prefetch=3,
            grid=(4,),
            in_specs=[
                pl.BlockSpec(
                    (1, HELD, 2, KV_WIDTH),
                    lambda i, where, ids, lengths: (ids[(where[1] + i) & 3], 0, 0, 0),
                ),
                IN_HBM,
            ],
            out_specs=[pl.BlockSpec((ROWS, HEAD_DIM), lambda i, *scalars: (0, 0))]
            + [pl.BlockSpec((HELD, PAIR), lambda i, *scalars: (0, 0))] * 4,
        ),
        out_shape=[jax.ShapeDtypeStruct((ROWS, HEAD_DIM), F32)]
        + [jax.ShapeDtypeStruct((HELD, PAIR), BF16)] * 4,
        compiler_params=params(),
        cost_estimate=cost(1, 1),
    )(where, ids, lengths, prefix_cache, gate)


def output_kernel(where, c0, c1, c2, c3, w0, w1, p0, p1, p2, p3, out, squares, held):
    step = pl.program_id(0)

    @pl.when(step == 0)
    def _():
        squares[...] = jnp.zeros_like(squares)

    for j, piece in enumerate((p0, p1, p2, p3)):
        lanes = pl.multiple_of(((where[1] - j) & 3) * HEAD_DIM, HEAD_DIM)
        for b in range(2):
            held[b, :, pl.ds(lanes, HEAD_DIM)] = piece[0, b]
    got = lax.dot_general(w0[...], c0[...], NT, preferred_element_type=F32)
    got += lax.dot_general(w1[...], c1[...], NT, preferred_element_type=F32)
    got += lax.dot_general(held[0], c2[...], NT, preferred_element_type=F32)
    got += lax.dot_general(held[1], c3[...], NT, preferred_element_type=F32)
    out[...] = got
    squares[...] += jnp.sum(got * got, 0, keepdims=True)


def output(where, contexts, weights, pieces):
    full = lambda shape: pl.BlockSpec(shape, lambda i, where: (0, 0))
    strip = pl.BlockSpec((STRIP, ROWS), lambda i, where: (i, 0))
    piece = pl.BlockSpec(
        (1, 2, STRIP, HEAD_DIM), lambda i, where: ((where[3] - i) & 3, 0, 0, 0)
    )
    return pl.pallas_call(
        output_kernel,
        grid_spec=pltpu.PrefetchScalarGridSpec(
            num_scalar_prefetch=1,
            grid=(4,),
            in_specs=[full((ROWS, 512))] * 4 + [strip] * 2 + [piece] * 4,
            out_specs=[strip, full((1, ROWS))],
            scratch_shapes=[pltpu.VMEM((2, STRIP, 512), BF16)],
        ),
        out_shape=[
            jax.ShapeDtypeStruct((FEATURES, ROWS), F32),
            jax.ShapeDtypeStruct((1, ROWS), F32),
        ],
        compiler_params=params(),
        cost_estimate=cost(4 * ROWS * 1024 * FEATURES, 8_000_000),
    )(where, *contexts, *weights, *pieces)


def rope_tables(places):
    lane = jnp.arange(HEAD_DIM)
    frequency = rope_base ** (-((lane % 64).astype(F32) * 2.0 / HEAD_DIM))
    angles = places * frequency[None, :]
    return jnp.cos(angles), jnp.where(lane[None, :] < 64, -jnp.sin(angles), jnp.sin(angles))


def shards(
    tokens,
    gain_pre,
    w_query,
    w_key,
    w_value,
    w_out,
    gain_post,
    prefix_cache,
    template_ids,
    prefix_lengths,
    doc_lengths,
):
    member = lax.axis_index("mp")
    place = lax.axis_index("seq")
    doc = place // DOC_SHARDS
    local = place % DOC_SHARDS
    where = jnp.stack(
        [member, doc, local, place % 4, place, member, member ^ 1, member ^ 2, member ^ 3]
    ).astype(jnp.int32)
    scalars = (where, template_ids, prefix_lengths)

    turned_tokens = tokens.T
    near = across_mp(turned_tokens, 1)
    far = across_mp(turned_tokens, 2)

    places, mine, *others = picked_rows(*scalars, prefix_cache, near)
    for by, other in enumerate(others, 1):
        mine = mine + along_x(other, by)
    prefix = jnp.stack([mine] + [z_flip(mine, flip) for flip in (1, 2, 3)])
    tables = rope_tables(places)

    piece_a, piece_b = turned_pieces(where, w_out, others[0])
    crossed = (across_mp(piece_a, 2), across_mp(piece_b, 3))

    gain = gain_pre.reshape(2 * MP, 1, STEP)
    weights = (w_query, w_key, w_value)
    carried = project(where, 0, [turned_tokens, near], gain, weights, (piece_a,))
    far, piece_a, piece_b, prefix, *_ = lax.optimization_barrier(
        (far, *crossed, prefix, *carried, *tables)
    )
    w_piece = jnp.stack([piece_a, piece_b])
    prefix_twin = to_twin(prefix)
    queries, own = project(
        where, 2, [far, across_mp(far, 1)], gain, weights, (), carried, tables
    )
    w_parts = [w_piece] + [along_z(w_piece, by) for by in (1, 2, 3)]
    one_back = within_doc(own, 1)
    two_back = within_doc(own, 2)
    w_parts = lax.optimization_barrier((*w_parts, own))[:4]
    w_line = jnp.stack(w_parts)
    w_next = along_x(w_line, 1)
    w_far = [w_line, w_next, along_x(w_next, 1), along_x(w_line, 3)]
    w_own, w_give = turned_weights(where, w_out, w_line)
    w_near = across_mp(w_give, 1)
    context = attention(
        (*scalars, doc_lengths), queries, own, one_back, two_back, (prefix, prefix_twin), (w_give,)
    )
    c_far = across_mp(context, 2)
    c_near = across_mp(context, 1)
    contexts = [context, c_near, c_far, across_mp(c_far, 1)]
    attended, own_squares = output(where, contexts, [w_own, w_near], w_far)
    total = own_squares
    for flip in (1, 2, 3):
        total = total + across_mp(own_squares, flip)
    scale = lax.rsqrt(total * (1.0 / (MP * FEATURES)) + epsilon)
    result = turned_tokens.astype(F32) + gain_post[:, None] * attended * scale
    return result.astype(BF16).T


def solution(mesh):
    placed = (
        P("seq", "mp"),
        P(),
        P(None, "mp"),
        P(None, "mp"),
        P(None, "mp"),
        P("mp", None),
        P("mp"),
        P(None, "seq", None, "mp"),
        P(),
        P(),
        P(),
    )
    return jax.shard_map(
        shards, mesh=mesh, in_specs=placed, out_specs=P("seq", "mp"), check_vma=False
    )
```

```python
import functools

import jax
import jax.numpy as jnp
from jax import lax
from jax.experimental import pallas as pl
from jax.experimental.pallas import tpu as pltpu
from jax.sharding import PartitionSpec as P

HEAD_DIM = 128
WINDOW = 1024
DOCS = 4
MP = 4
ROWS = 512
HALF = 256
FEATURES = 1344
STEP = 672
HEADS_LOCAL = 4
KV_WIDTH = 256
PAIR = 2 * KV_WIDTH
DOC_SHARDS = 8
HELD = 128
STRIP = FEATURES // 4
VMEM_LIMIT = 63 * 1024 * 1024

epsilon = 1e-06
query_scalar = 168.0
rope_base = 10000.0
F32 = jnp.float32
BF16 = jnp.bfloat16


def cost(flops, moved, exps=0):
    return pl.CostEstimate(flops=flops, bytes_accessed=moved, transcendentals=exps)


def params():
    return pltpu.CompilerParams(vmem_limit_bytes=VMEM_LIMIT)


def across_mp(array, flip):
    return lax.ppermute(array, "mp", [(i, i ^ flip) for i in range(MP)])


def seq_place(x, y_lo, z):
    return x * 8 + y_lo * 4 + z


def along_x(array, by):
    pairs = [
        (seq_place(x, y, z), seq_place((x + by) % 4, y, z))
        for x in range(4)
        for y in range(2)
        for z in range(4)
    ]
    return lax.ppermute(array, "seq", pairs)


def along_z(array, by):
    pairs = [
        (seq_place(x, y, z), seq_place(x, y, (z + by) % 4))
        for x in range(4)
        for y in range(2)
        for z in range(4)
    ]
    return lax.ppermute(array, "seq", pairs)


def to_twin(array):
    pairs = [(i, i ^ 4) for i in range(DOCS * DOC_SHARDS)]
    return lax.ppermute(array, "seq", pairs)


def z_flip(array, flip):
    return lax.ppermute(array, "seq", [(i, i ^ flip) for i in range(DOCS * DOC_SHARDS)])


def within_doc(array, by):
    pairs = [
        (d * DOC_SHARDS + i, d * DOC_SHARDS + (i + by) % DOC_SHARDS)
        for d in range(DOCS)
        for i in range(DOC_SHARDS)
    ]
    return lax.ppermute(array, "seq", pairs)


def after(array, *others):
    return lax.optimization_barrier((array, *others))[0]


TN = (((0,), (0,)), ((), ()))
NT = (((1,), (1,)), ((), ()))


IN_HBM = pl.BlockSpec(memory_space=pltpu.HBM)


def project_kernel(chunks, groups, first, kind, order, *refs):
    step = pl.program_id(0)
    count = sum(groups)
    xs, gain, weights = refs[:chunks], refs[chunks], refs[chunks + 1 : chunks + 1 + count]
    held = len(groups) + 1
    accs = refs[-held:]
    if kind:
        carried, cosine, sine, out = refs[-2 * held - 3 : -held - 3], *refs[-held - 3 : -held]
    else:
        carried = (None,) * held if first else refs[-2 * held : -held]

    for number in range(chunks):

        @pl.when(step // 2 == number)
        def _(number=number):
            x = jnp.transpose(xs[number][...]).astype(F32)
            scaled = (x * gain[0]).astype(BF16)
            parts = [jnp.dot(scaled, w[...], preferred_element_type=F32) for w in weights]
            square = jnp.broadcast_to(jnp.sum(x * x, 1, keepdims=True), accs[-1].shape)

            def put(sources):
                at = 0
                for group, acc, source in zip(groups, accs, sources):
                    left = 0
                    for part in parts[at : at + group]:
                        cols = slice(left, left + part.shape[1])
                        acc[:, cols] = part if source is None else source[:, cols] + part
                        left = cols.stop
                    at += group
                accs[-1][...] = square if sources[-1] is None else sources[-1][...] + square

            if number:
                put(accs)
            else:

                @pl.when(step == 0)
                def _():
                    put(carried)

                @pl.when(step == 1)
                def _():
                    put(accs)

    if kind:

        @pl.when(step == 2 * chunks - 1)
        def _():
            scale = lax.rsqrt(accs[-1][...] * (1.0 / (MP * FEATURES)) + epsilon)
            for head in range(4):
                cols = slice(head * HEAD_DIM, (head + 1) * HEAD_DIM)
                part = accs[0][:, cols] * scale
                if kind == "queries" or head < 2:
                    part = part * cosine[...] + pltpu.roll(part, 64, 1) * sine[...]
                if kind == "queries":
                    part = part * query_scalar ** (-0.5)
                out[:, cols] = part.astype(BF16)


def project(order, start, xs, gain, weights, groups, gates=(), carried=(), tables=(), kind=None):
    chunks = len(xs)
    full = lambda shape: pl.BlockSpec(shape, lambda i, order: (0,) * len(shape))
    at = lambda i, order: order[5 + start + i // 2] * 2 + i % 2
    acc_shapes = [(ROWS, 512)] * len(groups) + [(ROWS, HEAD_DIM)]
    if kind:
        out_shape = [jax.ShapeDtypeStruct((ROWS, 512), BF16)]
        scratch = [pltpu.VMEM(shape, F32) for shape in acc_shapes]
    else:
        out_shape = [jax.ShapeDtypeStruct(shape, F32) for shape in acc_shapes]
        scratch = []
    return pl.pallas_call(
        functools.partial(project_kernel, chunks, groups, not carried, kind),
        grid_spec=pltpu.PrefetchScalarGridSpec(
            num_scalar_prefetch=1,
            grid=(2 * chunks,),
            in_specs=[
                pl.BlockSpec((STEP, ROWS), lambda i, order, k=k: (jnp.clip(i - 2 * k, 0, 1), 0))
                for k in range(chunks)
            ]
            + [pl.BlockSpec((1, 1, STEP), lambda i, order: (at(i, order), 0, 0))]
            + [pl.BlockSpec((STEP, w.shape[1]), lambda i, order: (at(i, order), 0)) for w in weights]
            + [IN_HBM] * len(gates)
            + [full(one.shape) for one in (*carried, *tables)],
            out_specs=[full(one.shape) for one in out_shape],
            scratch_shapes=scratch,
        ),
        out_shape=out_shape,
        compiler_params=params(),
        cost_estimate=cost(3_000_000_000, 10_000_000) if kind else cost(1, 1),
    )(order, *xs, gain, *weights, *gates, *carried, *tables)


def attention_kernel(where, ids, lengths, reals, q_ref, own, one_back, two_back, *refs):
    prefix, twin, _, out, held, lines, sems = refs
    local = where[2]
    length = lengths[ids[where[1]]]
    real = reals[where[1]]

    def fetch(pairs):
        copies = [pltpu.make_async_copy(a, b, sems.at[i]) for i, (a, b) in enumerate(pairs)]
        for one in copies:
            one.start()
        for one in copies:
            one.wait()

    def fetch_prefix():
        fetch(
            [
                (
                    source.at[r],
                    lines.at[side, pl.ds(pl.multiple_of((where[3] ^ r) * HELD, HELD), HELD)],
                )
                for side, source in enumerate((prefix, twin))
                for r in range(4)
            ]
        )

    def picked(late_part):
        row = lax.broadcasted_iota(jnp.int32, (ROWS, 1), 0)
        late = ((row - length) & (WINDOW - 1)) >= ROWS
        low = lines[0].astype(F32)
        high = lines[1].astype(F32)
        return (jnp.where(late, low, high) if late_part else jnp.where(late, high, low)).astype(
            BF16
        )

    @pl.when(local == 0)
    def _():
        fetch_prefix()
        held[:ROWS] = picked(False)
        held[ROWS:] = picked(True)

    @pl.when(local == 1)
    def _():
        fetch_prefix()
        held[:ROWS] = picked(True)
        fetch([(one_back, held.at[pl.ds(ROWS, ROWS)])])

    @pl.when(local >= 2)
    def _():
        fetch([(two_back, held.at[pl.ds(0, ROWS)]), (one_back, held.at[pl.ds(ROWS, ROWS)])])

    column = lax.broadcasted_iota(jnp.int32, (1, ROWS), 1)
    shift_two = jnp.where(local < 2, length, 0)
    limit_two = jnp.where(local < 2, WINDOW - ROWS * local - length, 0)
    shift_one = jnp.where(local < 1, length, 0)
    limit_one = jnp.where(local < 1, ROWS - length, 0)
    place_two = (column - shift_two) & (ROWS - 1)
    place_one = (column - shift_one) & (ROWS - 1)
    one_ok = place_one >= limit_one
    for half in range(2):
        mine = slice(half * HALF, (half + 1) * HALF)
        row = half * HALF + (lax.broadcasted_iota(jnp.int32, (2 * HALF, 1), 0) & (HALF - 1))
        two_ok = place_two > jnp.maximum(row, limit_two - 1)
        own_ok = column[:, mine] <= row
        row_real = row + local * ROWS < real
        for head in range(2):
            k_cols = slice(head * HEAD_DIM, (head + 1) * HEAD_DIM)
            v_cols = slice(KV_WIDTH + k_cols.start, KV_WIDTH + k_cols.stop)
            firsts = [(2 * head + i) * HEAD_DIM for i in range(2)]
            q = jnp.concatenate([q_ref[mine, at : at + HEAD_DIM] for at in firsts], 0)
            parts = [
                (two_ok, held[:ROWS, k_cols], held[:ROWS, v_cols]),
                (one_ok, held[ROWS:, k_cols], held[ROWS:, v_cols]),
            ]
            if half:
                parts.append((None, own[:HALF, k_cols], own[:HALF, v_cols]))
            parts.append((own_ok, own[mine, k_cols], own[mine, v_cols]))
            scores = []
            for ok, keys, _ in parts:
                s = lax.dot_general(q, keys, NT, preferred_element_type=F32)
                scores.append(s if ok is None else jnp.where(ok, s, -1e30))
            top = functools.reduce(jnp.maximum, [jnp.max(s, 1, keepdims=True) for s in scores])
            total = 0.0
            got = 0.0
            for s, (_, _, values) in zip(scores, parts):
                weights = jnp.exp(s - top)
                total += jnp.sum(weights, 1, keepdims=True)
                got += jnp.dot(weights.astype(BF16), values, preferred_element_type=F32)
            got = jnp.where(row_real, got / total, 0.0).astype(BF16)
            for i, at in enumerate(firsts):
                out[mine, at : at + HEAD_DIM] = got[i * HALF : (i + 1) * HALF]


def attention(scalars, q, own, one_back, two_back, prefix, gates):
    full = pl.BlockSpec((ROWS, 512), lambda i, *scalars: (0, 0))
    return pl.pallas_call(
        attention_kernel,
        grid_spec=pltpu.PrefetchScalarGridSpec(
            num_scalar_prefetch=4,
            grid=(1,),
            in_specs=[full] * 2 + [IN_HBM] * 5,
            out_specs=full,
            scratch_shapes=[
                pltpu.VMEM((2 * ROWS, PAIR), BF16),
                pltpu.VMEM((2, ROWS, PAIR), BF16),
                pltpu.SemaphoreType.DMA((8,)),
            ],
        ),
        out_shape=jax.ShapeDtypeStruct((ROWS, 512), BF16),
        compiler_params=params(),
        cost_estimate=cost(1, 1),
    )(*scalars, q, own, one_back, two_back, *prefix, *gates)


def piece_kernel(where, w_ref, gate, piece_a, piece_b, turned):
    strip = pl.ds(pl.multiple_of(where[3] * STRIP, 16), STRIP)
    for m in range(MP):

        @pl.when(where[0] == m)
        def _(m=m):
            for flip, piece in ((2, piece_a), (3, piece_b)):
                at = (m ^ flip) * FEATURES
                turned[...] = jnp.transpose(w_ref[:, at : at + FEATURES])
                piece[...] = turned[strip, :]


def turned_pieces(where, w_out, gate):
    piece = pl.BlockSpec((STRIP, 128), lambda i, where: (0, 0))
    return pl.pallas_call(
        piece_kernel,
        grid_spec=pltpu.PrefetchScalarGridSpec(
            num_scalar_prefetch=1,
            grid=(1,),
            in_specs=[pl.BlockSpec((128, MP * FEATURES), lambda i, where: (where[1], 0)), IN_HBM],
            out_specs=[piece, piece],
            scratch_shapes=[pltpu.VMEM((FEATURES, 128), BF16)],
        ),
        out_shape=[jax.ShapeDtypeStruct((STRIP, 128), BF16)] * 2,
        compiler_params=params(),
        cost_estimate=cost(1, 1),
    )(where, w_out, gate)


def turn_kernel(where, w_ref, gate, own, near):
    for m in range(MP):

        @pl.when(where[0] == m)
        def _(m=m):
            for flip, out in ((0, own), (1, near)):
                at = (m ^ flip) * FEATURES
                out[...] = jnp.transpose(w_ref[:, at : at + FEATURES])


def turned_weights(where, w_out, gate):
    whole = pl.BlockSpec((FEATURES, 128), lambda i, where: (0, i))
    return pl.pallas_call(
        turn_kernel,
        grid_spec=pltpu.PrefetchScalarGridSpec(
            num_scalar_prefetch=1,
            grid=(4,),
            in_specs=[pl.BlockSpec((128, MP * FEATURES), lambda i, where: (i, 0)), IN_HBM],
            out_specs=[whole, whole],
        ),
        out_shape=[jax.ShapeDtypeStruct((FEATURES, 512), BF16)] * 2,
        compiler_params=params(),
        cost_estimate=cost(1, 1),
    )(where, w_out, gate)


def pick_kernel(where, ids, lengths, rows_ref, gate, places, *outs):
    step = pl.program_id(0)

    @pl.when(step == 0)
    def _():
        first = lengths[ids[where[1]]] + where[2] * ROWS
        row = lax.broadcasted_iota(jnp.int32, (ROWS, HEAD_DIM), 0)
        places[...] = (row + first).astype(F32)

    reach = lengths[ids[(where[1] + step) & 3]]
    held_at = where[4] * HELD + lax.broadcasted_iota(jnp.int32, (HELD, 1), 0)
    wanted = (held_at < reach) & (held_at >= reach - WINDOW)
    for number, out in enumerate(outs):

        @pl.when(step == number)
        def _(out=out):
            for part in range(2):
                rows = rows_ref[0, :, part, :].astype(F32)
                out[:, part * KV_WIDTH : (part + 1) * KV_WIDTH] = jnp.where(
                    wanted, rows, 0.0
                ).astype(BF16)


def picked_rows(where, ids, lengths, prefix_cache, gate):
    return pl.pallas_call(
        pick_kernel,
        grid_spec=pltpu.PrefetchScalarGridSpec(
            num_scalar_prefetch=3,
            grid=(4,),
            in_specs=[
                pl.BlockSpec(
                    (1, HELD, 2, KV_WIDTH),
                    lambda i, where, ids, lengths: (ids[(where[1] + i) & 3], 0, 0, 0),
                ),
                IN_HBM,
            ],
            out_specs=[pl.BlockSpec((ROWS, HEAD_DIM), lambda i, *scalars: (0, 0))]
            + [pl.BlockSpec((HELD, PAIR), lambda i, *scalars: (0, 0))] * 4,
        ),
        out_shape=[jax.ShapeDtypeStruct((ROWS, HEAD_DIM), F32)]
        + [jax.ShapeDtypeStruct((HELD, PAIR), BF16)] * 4,
        compiler_params=params(),
        cost_estimate=cost(1, 1),
    )(where, ids, lengths, prefix_cache, gate)


def output_kernel(where, c0, c1, c2, c3, w0, w1, p0, p1, p2, p3, out, squares, held):
    step = pl.program_id(0)

    @pl.when(step == 0)
    def _():
        squares[...] = jnp.zeros_like(squares)

    for j, piece in enumerate((p0, p1, p2, p3)):
        lanes = pl.multiple_of(((where[1] - j) & 3) * HEAD_DIM, HEAD_DIM)
        for b in range(2):
            held[b, :, pl.ds(lanes, HEAD_DIM)] = piece[0, b]
    got = lax.dot_general(w0[...], c0[...], NT, preferred_element_type=F32)
    got += lax.dot_general(w1[...], c1[...], NT, preferred_element_type=F32)
    got += lax.dot_general(held[0], c2[...], NT, preferred_element_type=F32)
    got += lax.dot_general(held[1], c3[...], NT, preferred_element_type=F32)
    out[...] = got
    squares[...] += jnp.sum(got * got, 0, keepdims=True)


def output(where, contexts, weights, pieces):
    full = lambda shape: pl.BlockSpec(shape, lambda i, where: (0, 0))
    strip = pl.BlockSpec((STRIP, ROWS), lambda i, where: (i, 0))
    piece = pl.BlockSpec(
        (1, 2, STRIP, HEAD_DIM), lambda i, where: ((where[3] - i) & 3, 0, 0, 0)
    )
    return pl.pallas_call(
        output_kernel,
        grid_spec=pltpu.PrefetchScalarGridSpec(
            num_scalar_prefetch=1,
            grid=(4,),
            in_specs=[full((ROWS, 512))] * 4 + [strip] * 2 + [piece] * 4,
            out_specs=[strip, full((1, ROWS))],
            scratch_shapes=[pltpu.VMEM((2, STRIP, 512), BF16)],
        ),
        out_shape=[
            jax.ShapeDtypeStruct((FEATURES, ROWS), F32),
            jax.ShapeDtypeStruct((1, ROWS), F32),
        ],
        compiler_params=params(),
        cost_estimate=cost(4 * ROWS * 1024 * FEATURES, 8_000_000),
    )(where, *contexts, *weights, *pieces)


def rope_tables(places):
    lane = jnp.arange(HEAD_DIM)
    frequency = rope_base ** (-((lane % 64).astype(F32) * 2.0 / HEAD_DIM))
    angles = places * frequency[None, :]
    return jnp.cos(angles), jnp.where(lane[None, :] < 64, -jnp.sin(angles), jnp.sin(angles))


def shards(
    tokens,
    gain_pre,
    w_query,
    w_key,
    w_value,
    w_out,
    gain_post,
    prefix_cache,
    template_ids,
    prefix_lengths,
    doc_lengths,
):
    member = lax.axis_index("mp")
    place = lax.axis_index("seq")
    doc = place // DOC_SHARDS
    local = place % DOC_SHARDS
    where = jnp.stack(
        [member, doc, local, place % 4, place, member, member ^ 1, member ^ 2, member ^ 3]
    ).astype(jnp.int32)
    scalars = (where, template_ids, prefix_lengths)

    turned_tokens = tokens.T
    near = across_mp(turned_tokens, 1)
    far = across_mp(turned_tokens, 2)

    places, mine, *others = picked_rows(*scalars, prefix_cache, near)
    for by, other in enumerate(others, 1):
        mine = mine + along_x(other, by)
    tables = rope_tables(places)

    piece_a, piece_b = turned_pieces(where, w_out, others[0])
    crossed = (across_mp(piece_a, 2), across_mp(piece_b, 3))

    gain = gain_pre.reshape(2 * MP, 1, STEP)
    carried = project(
        where,
        0,
        [turned_tokens, near],
        gain,
        (w_query, w_key, w_value),
        (1, 2),
        (piece_a,),
    )
    mine = after(mine, carried[2])
    prefix_parts = [mine] + [z_flip(mine, flip) for flip in (1, 2, 3)]
    far, *parts = lax.optimization_barrier((far, *crossed, *prefix_parts, *carried, *tables))
    w_piece = jnp.stack(parts[:2])
    prefix = jnp.stack(parts[2:6])
    prefix_twin = to_twin(prefix)
    w_parts = [w_piece] + [along_z(w_piece, by) for by in (1, 2, 3)]
    fars = [far, across_mp(far, 1)]
    (own,) = project(
        where, 2, fars, gain, (w_key, w_value), (2,), (), carried[1:], tables, "keys"
    )
    one_back = within_doc(own, 1)
    two_back = within_doc(own, 2)
    (queries,) = project(
        where, 2, fars, gain, (w_query,), (1,), (own,), carried[::2], tables, "queries"
    )

    w_line = jnp.stack(lax.optimization_barrier((*w_parts, queries))[:4])
    w_next = along_x(w_line, 1)
    w_far = [w_line, w_next, along_x(w_next, 1), along_x(w_line, 3)]
    w_own, w_give = turned_weights(where, w_out, w_line)
    w_near = across_mp(w_give, 1)
    context = attention(
        (*scalars, doc_lengths), queries, own, one_back, two_back, (prefix, prefix_twin), (w_give,)
    )
    c_far = across_mp(context, 2)
    c_near = across_mp(context, 1)
    contexts = [context, c_near, c_far, across_mp(c_far, 1)]
    attended, own_squares = output(where, contexts, [w_own, w_near], w_far)
    total = own_squares
    for flip in (1, 2, 3):
        total = total + across_mp(own_squares, flip)
    scale = lax.rsqrt(total * (1.0 / (MP * FEATURES)) + epsilon)
    result = turned_tokens.astype(F32) + gain_post[:, None] * attended * scale
    return result.astype(BF16).T


def solution(mesh):
    placed = (
        P("seq", "mp"),
        P(),
        P(None, "mp"),
        P(None, "mp"),
        P(None, "mp"),
        P("mp", None),
        P("mp"),
        P(None, "seq", None, "mp"),
        P(),
        P(),
        P(),
    )
    return jax.shard_map(
        shards, mesh=mesh, in_specs=placed, out_specs=P("seq", "mp"), check_vma=False
    )
```
